512 devices in a mesh: gx: 32 (over z, core), gy: 16 (over y, x).
Axes of the slice: x: 4, y: 4, z: 16, core: 2. Of those that a mesh axis runs over, the one named last changes fastest.
Arguments:
- loads: bfloat16 [32, 16, 384, 128], P('gx', 'gy'), may hold values from -6 to 6
- schur: bfloat16 [32, 16, 768, 768], P('gx', 'gy'), as said below
- local_inv: bfloat16 [32, 16, 768, 768], P('gx', 'gy'), as said below
- coarse_basis: bfloat16 [32, 16, 12, 768], P('gx', 'gy'), may hold values from -0.21875 to 0.21875
- coarse_index: int32 [32, 16, 12], P('gx', 'gy'), may hold values from 0 to 3071, as said below
- face_nodes: int32 [32, 16, 2], P('gx', 'gy'), may hold values from 16 to 64, as said below
- coarse_inverse: float32 [3072, 3072], P('gy', 'gx'), as said below
Outputs:
- solution: float32 [32, 16, 384, 128], P('gx', 'gy')
- preconditioned: float32 [32, 16, 384, 128], P('gx', 'gy')
The draws below stay inside these ranges and needn't reach their ends.
Inputs may be any that keep to these rules, and one draw needn't show every extreme that they name: `face_nodes`: live nodes of each owned face; the faces on the slab's outer edge are clamped whatever the count says. Some face has all 64 nodes. For c < 3, coarse_index[a, b, 3 + c] and coarse_index[a, b, 9 + c] number the averages of the east and north faces of (a, b); coarse_index[a, b, c] = coarse_index[a - 1, b, 3 + c] and coarse_index[a, b, 6 + c] = coarse_index[a, b - 1, 9 + c], with a - 1 taken modulo 32 and b - 1 modulo 16. Every coarse unknown is named by exactly two primal unknowns. `schur`: symmetric positive definite. `local_inv`: symmetric positive definite. `coarse_inverse`: symmetric positive definite.
All inputs are finite; a program needn't handle non-finite values.
Results may differ from the reference program's by a relative error of at most 0.024.
Values may be sent and summed in bfloat16 or wider, within the bound.
A program may use at most 64 MiB of HBM per device.

```python
import math
import jax
import jax.numpy as jnp
from jax import lax

NODES = 64
FACE = 192
LOCAL = 768
NRHS = 128
NP = 12
ITERS = 2
SUB_X = 32
SUB_Y = 16
NC = 3072


def dominant(key, number, order, lowest, highest):

    def single(position):
        subkey = jax.random.fold_in(key, position)
        key_one, key_two = jax.random.split(subkey)
        entries = jax.random.uniform(key_one, (order, order), jnp.float32, -1.0, 1.0)
        coupled = (entries + entries.T) * (1.25 / math.sqrt(order))
        scales = jnp.exp(jax.random.uniform(key_two, (order,), jnp.float32, math.log(lowest), math.log(highest)))
        unit_diag = jnp.eye(order, dtype=jnp.float32)
        return coupled * (1.0 - unit_diag) + unit_diag * scales[:, None]
    return lax.map(single, jnp.arange(number))


def draw_schur(key, part):
    key = jax.random.fold_in(key, 11)
    blocks = dominant(key, SUB_X * SUB_Y, LOCAL, 3.0, 9.0)
    return blocks.reshape(SUB_X, SUB_Y, LOCAL, LOCAL).astype(jnp.bfloat16)


def draw_local_inv(key, part):
    key = jax.random.fold_in(key, 23)
    blocks = dominant(key, SUB_X * SUB_Y, LOCAL, 3.0, 9.0)
    return (0.5 * blocks).reshape(SUB_X, SUB_Y, LOCAL, LOCAL).astype(jnp.bfloat16)


def draw_coarse_inverse(key, part):
    key = jax.random.fold_in(key, 37)
    blocks = dominant(key, 1, NC, 3.0, 9.0)
    return 2.5 * blocks[0]


def draw_face_nodes(key, part):
    key = jax.random.fold_in(key, 41)
    counts = jax.random.randint(key, (SUB_X, SUB_Y, 2), NODES // 4, NODES + 1, dtype=jnp.int32)
    return counts.at[0, 0, 0].set(NODES)


def draw_coarse_index(key, part):
    key = jax.random.fold_in(key, 53)
    order = jax.random.permutation(key, jnp.arange(NC, dtype=jnp.int32))
    rows = jnp.arange(SUB_X, dtype=jnp.int32)[:, None]
    cols = jnp.arange(SUB_Y, dtype=jnp.int32)[None, :]
    own_slot = 6 * (rows * SUB_Y + cols)
    west_slot = 6 * ((rows - 1) % SUB_X * SUB_Y + cols)
    south_slot = 6 * (rows * SUB_Y + (cols - 1) % SUB_Y) + 3
    north_slot = own_slot + 3
    component = jnp.arange(3, dtype=jnp.int32)
    slots = jnp.concatenate([west_slot[..., None] + component, own_slot[..., None] + component, south_slot[..., None] + component, north_slot[..., None] + component], axis=2)
    return jnp.take(order, slots.reshape(-1)).reshape(SUB_X, SUB_Y, 12).astype(jnp.int32)


def levels(key, extent, shards, least, largest):
    def one(axis_at, parts):
        heights = jax.random.uniform(jax.random.fold_in(jax.random.fold_in(key, 6), axis_at), (parts,), jnp.float32, least / len(shards), largest / len(shards))
        return jnp.repeat(jnp.exp(heights), extent[axis_at] // parts).reshape((-1,) + (1,) * (len(extent) - axis_at - 1))

    gain = one(*shards[0])
    for cut in shards[1:]:
        gain = gain * one(*cut)
    return gain


def scatter_about(rng, shape, deviation, reach, pieces=(), held_as=jnp.bfloat16):
    loudness = levels(rng, shape, pieces, -0.22, 0.18) if pieces else 1.0
    values = jax.random.normal(rng, shape, jnp.float32) * deviation * loudness
    return jnp.minimum(jnp.maximum(values, -reach), reach).astype(held_as)


def setup_inputs(seed: int = 0) -> dict:
    key_of = jax.random.split(jax.random.key(seed), 8)
    loads = scatter_about(key_of[0], (SUB_X, SUB_Y, 2 * FACE, NRHS), 1.0, 6.0, ((0, 32), (1, 16)))
    schur = draw_schur(jax.random.fold_in(key_of[7], 71), 0)
    local_inv = draw_local_inv(jax.random.fold_in(key_of[7], 71), 0)
    coarse_basis = scatter_about(key_of[3], (SUB_X, SUB_Y, NP, LOCAL), LOCAL ** -0.5, 0.21875, ((0, 32), (1, 16)))
    coarse_index = draw_coarse_index(jax.random.fold_in(key_of[7], 71), 0)
    face_nodes = draw_face_nodes(jax.random.fold_in(key_of[7], 71), 0)
    coarse_inverse = draw_coarse_inverse(jax.random.fold_in(key_of[7], 71), 0)
    return {"loads": loads, "schur": schur, "local_inv": local_inv, "coarse_basis": coarse_basis, "coarse_index": coarse_index, "face_nodes": face_nodes, "coarse_inverse": coarse_inverse}


def restrict(vector):
    east_face = vector[:, :, :FACE]
    north_face = vector[:, :, FACE:]
    west_face = jnp.concatenate([jnp.zeros_like(east_face[:1]), east_face[:-1]], axis=0)
    south_face = jnp.concatenate([jnp.zeros_like(north_face[:, :1]), north_face[:, :-1]], axis=1)
    return jnp.concatenate([west_face, east_face, south_face, north_face], axis=2)


def extend(local_vals, live_mask):
    west_rows = local_vals[:, :, :FACE]
    south_rows = local_vals[:, :, 2 * FACE:3 * FACE]
    from_right = jnp.concatenate([west_rows[1:], jnp.zeros_like(west_rows[:1])], axis=0)
    from_above = jnp.concatenate([south_rows[:, 1:], jnp.zeros_like(south_rows[:, :1])], axis=1)
    east_face = local_vals[:, :, FACE:2 * FACE] + from_right
    north_face = local_vals[:, :, 3 * FACE:] + from_above
    return jnp.concatenate([east_face, north_face], axis=2) * live_mask


def apply_blocks(matrices, local_vals):
    flat_mats = matrices.reshape(-1, LOCAL, LOCAL)
    flat_rows = local_vals.reshape(-1, LOCAL, NRHS)

    def product(operands):
        return jnp.dot(operands[0], operands[1], preferred_element_type=jnp.float32)

    result = lax.map(product, (flat_mats, flat_rows))
    return result.reshape(SUB_X, SUB_Y, LOCAL, NRHS)


def reference(loads, schur, local_inv, coarse_basis, coarse_index, face_nodes, coarse_inverse):
    highest = lax.Precision.HIGHEST
    node_of = jnp.arange(FACE) % NODES
    live_nodes = node_of[None, None, None, :] < face_nodes[..., None]
    inside_x = jnp.broadcast_to((jnp.arange(SUB_X) < SUB_X - 1)[:, None], (SUB_X, SUB_Y))
    inside_y = jnp.broadcast_to((jnp.arange(SUB_Y) < SUB_Y - 1)[None, :], (SUB_X, SUB_Y))
    inside = jnp.stack([inside_x, inside_y], axis=2)
    live_mask = (live_nodes & inside[..., None]).astype(jnp.float32).reshape(SUB_X, SUB_Y, 2 * FACE, 1)
    basis_wide = coarse_basis.astype(jnp.float32)
    flat_index = coarse_index.reshape(-1).astype(jnp.int32)

    def operate(direction):
        local_rows = restrict(direction.astype(jnp.bfloat16))
        return extend(apply_blocks(schur, local_rows), live_mask)

    def precondition(residual):
        local_rows = restrict(residual.astype(jnp.bfloat16))
        local_part = apply_blocks(local_inv, local_rows)
        primal = jnp.einsum("xypl,xyln->xypn", basis_wide, local_rows.astype(jnp.float32), precision=highest)
        coarse_rhs = jax.ops.segment_sum(primal.reshape(-1, NRHS), flat_index, num_segments=NC)
        coarse_sol = jnp.dot(coarse_inverse, coarse_rhs, precision=highest)
        picked = jnp.take(coarse_sol, flat_index, axis=0).reshape(SUB_X, SUB_Y, NP, NRHS).astype(jnp.bfloat16)
        spread = jnp.einsum("xypl,xypn->xyln", basis_wide, picked.astype(jnp.float32), precision=highest)
        return extend(local_part + spread, live_mask)

    def inner_product(first_arr, second_arr):
        return jnp.sum(first_arr * second_arr, axis=(0, 1, 2))

    residual = loads.astype(jnp.float32) * live_mask
    solution = jnp.zeros_like(residual)
    precond = precondition(residual)
    direction = precond
    current = inner_product(residual, precond)
    for iteration in range(ITERS):
        mapped = operate(direction)
        step_size = current / inner_product(direction, mapped)
        solution = solution + step_size * direction
        residual = residual - step_size * mapped
        precond = precondition(residual)
        updated = inner_product(residual, precond)
        direction = precond + (updated / current) * direction
        current = updated
    return solution, precond
```

```python
import functools
import jax
import jax.numpy as jnp
from jax import lax
from jax.experimental import pallas as pl
from jax.experimental.pallas import tpu as pltpu
from jax.sharding import PartitionSpec as P

MESH = pl.DeviceIdType.MESH
F32 = jnp.float32
BF16 = jnp.bfloat16
TILE = 16
CODE = 4096
MASK_LANE = 64
BT_LANES = 128
SOLVES = 3
OPS = 2


def kernel(
    n_gx,
    n_gy,
    loads,
    schur_hbm,
    linv_hbm,
    basis,
    index,
    nodes,
    cinv,
    sol_out,
    pre_out,
    schur,
    linv,
    bpad,
    bt_send,
    bt_recv,
    bb,
    masks,
    rows,
    name_msg,
    name_plane,
    name_gx,
    sel_t,
    strip,
    tsel,
    c2,
    t_val,
    t_send,
    t_recv,
    s_send,
    s_recv,
    g_msg,
    g_buf,
    xs,
    xr,
    x_msg,
    xb,
    ys,
    yr,
    pk,
    v0,
    v1,
    z1,
    w0,
    load_sem,
    face_send,
    face_recv,
    name_send,
    name_recv,
    strip_send,
    strip_recv,
    c2_send,
    c2_recv,
    stage_send,
    stage_recv,
    t_ssem,
    t_rsem,
    s_ssem,
    s_rsem,
    p_ssem,
    p_rsem,
):
    a = lax.axis_index("gx")
    b = lax.axis_index("gy")
    n_z = n_gx // 2
    n_plane = 2 * n_gy
    z = a // 2
    c = lax.rem(a, 2)
    slot = c * n_gy + b
    local = schur.shape[0]
    face = local // 4
    nodes_per = face // 3
    cr, cc = cinv.shape
    strip_w = 8 * n_gy
    nc = cr * n_gy
    load_cases = loads.shape[1]

    def plane_peer(k):
        other = lax.rem(slot + k, n_plane)
        return {"gx": 2 * z + other // n_gy, "gy": lax.rem(other, n_gy)}

    def signal(device):
        pl.semaphore_signal(barrier, inc=1, device_id=device, device_id_type=MESH)

    barrier = pltpu.get_barrier_semaphore()

    @pl.loop(1, n_plane)
    def _(k):
        signal(plane_peer(k))

    @pl.loop(1, n_gx)
    def _(k):
        other = lax.rem(a + k, n_gx)

        @pl.when(other // 2 != z)
        def _():
            signal({"gx": other, "gy": b})

    load_linv = pltpu.make_async_copy(linv_hbm, linv, load_sem.at[0])
    load_schur = pltpu.make_async_copy(schur_hbm, schur, load_sem.at[1])
    load_linv.start()
    load_schur.start()

    def remote(src, dst, send, recv, device):
        return pltpu.make_async_remote_copy(
            src_ref=src,
            dst_ref=dst,
            send_sem=send,
            recv_sem=recv,
            device_id=device,
            device_id_type=MESH,
        )

    def plane_send(src, dst, send, recv):
        @pl.loop(1, n_plane)
        def _(k):
            remote(src, dst.at[slot], send, recv, plane_peer(k)).start()

    def z_send(src, dst, send, recv):
        @pl.loop(1, n_z)
        def _(k):
            other = lax.rem(z + k, n_z)
            remote(
                src.at[other], dst.at[z], send, recv, {"gx": 2 * other + c, "gy": b}
            ).start()

    def wait_bytes(buf, count, sem):
        part = buf.at[pl.ds(0, count)]
        pltpu.make_async_copy(part, part, sem).wait()

    west = {"gx": lax.rem(a + n_gx - 1, n_gx), "gy": b}
    east = {"gx": lax.rem(a + 1, n_gx), "gy": b}
    south = {"gx": a, "gy": lax.rem(b + n_gy - 1, n_gy)}
    north = {"gx": a, "gy": lax.rem(b + 1, n_gy)}
    neighbours = ((west, 1), (east, 0), (south, 3), (north, 2))

    def face_rows(which):
        return pl.ds(which * face, face)

    def exchange(src, dst, send, recv):
        copies = []
        for mine, (device, theirs) in enumerate(neighbours):
            copies.append(
                remote(
                    src.at[face_rows(mine)],
                    dst.at[face_rows(theirs)],
                    send.at[mine],
                    recv.at[theirs],
                    device,
                )
            )
        for copy in copies:
            copy.start()
        return copies

    def finish(copies):
        for copy in copies:
            copy.wait_recv()

    lane = lax.broadcasted_iota(jnp.int32, (1, local), 1)
    which = lane // face
    node = lax.rem(lax.rem(lane, face), nodes_per)
    alive_east = (which == 1) & (node < nodes[0]) & (a < n_gx - 1)
    alive_north = (which == 3) & (node < nodes[1]) & (b < n_gy - 1)
    mask_row = jnp.where(alive_east | alive_north, 1.0, 0.0).astype(F32)
    basis_wide = basis[...].astype(F32)
    n_primal = basis_wide.shape[0]

    bpad[...] = jnp.zeros_like(bpad)
    bpad[TILE : TILE + n_primal, :] = basis_wide
    bpad[MASK_LANE : MASK_LANE + 1, :] = mask_row
    flipped = bpad[...].T
    bt_send[...] = flipped.astype(BF16)
    masks[...] = jnp.broadcast_to(flipped[:, MASK_LANE : MASK_LANE + 1], masks.shape)
    bpad[...] = jnp.zeros_like(bpad)
    bpad[0:n_primal, :] = basis_wide
    bb[...] = bpad[...].T.astype(BF16)
    basis16 = bpad[0:TILE, :].astype(BF16)

    rows[face : 2 * face, :] = (
        loads[0:face, :].astype(F32) * masks[face : 2 * face, :]
    ).astype(BF16)
    rows[3 * face :, :] = (
        loads[face:, :].astype(F32) * masks[3 * face :, :]
    ).astype(BF16)

    name_row = lax.broadcasted_iota(jnp.int32, name_msg.shape, 0)
    name_lane = lax.broadcasted_iota(jnp.int32, name_msg.shape, 1)
    names = CODE + name_row - n_primal
    for j in range(n_primal):
        names = jnp.where(name_row == j, index[j], names)
    half = name_msg.shape[1] // 2
    name_msg[...] = (
        jnp.where(name_lane < half, names // 64, lax.rem(names, 64)).astype(F32).astype(BF16)
    )
    name_plane[slot] = name_msg[...]
    name_gx[c * n_z + z] = name_msg[...]

    my_strip = strip.at[pl.ds(pl.multiple_of(b * cr, 8), cr)]
    wide = jnp.concatenate(
        [cinv[...].astype(BF16), jnp.zeros((cr, strip_w - cc), BF16)], axis=1
    )
    strip[pl.ds(pl.multiple_of(b * cr, 8), cr), :] = wide

    pl.semaphore_wait(barrier, n_plane - 1 + n_gx - 2)

    start_copies = []
    for mine, (device, theirs) in ((1, (east, 0)), (3, (north, 2))):
        copy = remote(
            rows.at[face_rows(mine)],
            rows.at[face_rows(theirs)],
            face_send.at[mine],
            face_recv.at[theirs],
            device,
        )
        copy.start()
        start_copies.append(copy)

    plane_send(name_msg, name_plane, name_send.at[0], name_recv.at[0])

    @pl.loop(1, n_gx)
    def _(k):
        other = lax.rem(a + k, n_gx)
        remote(
            name_msg,
            name_gx.at[c * n_z + z],
            name_send.at[1],
            name_recv.at[1],
            {"gx": other, "gy": b},
        ).start()

    @pl.loop(1, n_gy)
    def _(k):
        other = lax.rem(b + k, n_gy)
        remote(my_strip, my_strip, strip_send, strip_recv, {"gx": a, "gy": other}).start()

    bt_copies = exchange(bt_send, bt_recv, face_send.at[pl.ds(4, 4)], face_recv.at[pl.ds(4, 4)])

    def coarse_start(k, local_rows, sums):
        primal = jnp.dot(basis16, local_rows, preferred_element_type=F32)
        for j, value in enumerate(sums):
            at = lax.broadcasted_iota(jnp.int32, primal.shape, 0) == n_primal + j
            primal = jnp.where(at, value, primal)
        message = primal.astype(BF16)
        g_msg[k] = message
        g_buf[k, slot] = message
        plane_send(g_msg.at[k], g_buf.at[k], stage_send.at[k, 0], stage_recv.at[k, 0])
        t_val[...] = jnp.dot(linv[...], local_rows, preferred_element_type=F32)
        t_send[k] = t_val[...].astype(BF16)
        return exchange(t_send.at[k], t_recv.at[k], t_ssem.at[k], t_rsem.at[k])

    def coarse_scatter(k):
        wait_bytes(g_buf.at[k], n_plane - 1, stage_recv.at[k, 0])
        gathered = g_buf[k].reshape(n_plane * TILE, load_cases)
        part = jnp.dot(sel_t[...], gathered, preferred_element_type=F32)
        part = part.reshape(n_z, 8, load_cases)
        xs[k] = part
        xr[k, z] = xs[k, z]
        z_send(xs.at[k], xr.at[k], stage_send.at[k, 1], stage_recv.at[k, 1])

    def coarse_gather(k):
        wait_bytes(xr.at[k], n_z - 1, stage_recv.at[k, 1])
        mine = jnp.sum(xr[k], axis=0)
        x_msg[k] = mine
        xb[k, slot] = mine
        plane_send(x_msg.at[k], xb.at[k], stage_send.at[k, 2], stage_recv.at[k, 2])

    def coarse_solve(k):
        wait_bytes(xb.at[k], n_plane - 1, stage_recv.at[k, 2])
        low = xb[k, 0:n_gy].reshape(strip_w, load_cases).astype(BF16)
        high = xb[k, n_gy:].reshape(strip_w, load_cases).astype(BF16)
        part = jnp.dot(c2[0], low, preferred_element_type=F32) + jnp.dot(
            c2[1], high, preferred_element_type=F32
        )
        ys[k] = part.astype(BF16).reshape(n_z, TILE, load_cases)
        yr[k, z] = ys[k, z]
        z_send(ys.at[k], yr.at[k], stage_send.at[k, 3], stage_recv.at[k, 3])

    def sums_of(k):
        both = xb[k, cc // 8]
        return [both[j : j + 1, :] for j in range(4)]

    def coarse_finish(k):
        wait_bytes(yr.at[k], n_z - 1, stage_recv.at[k, 3])
        picked = jnp.sum(yr[k].astype(F32), axis=0).astype(BF16)
        for at in range(4):
            pk[k, at, 0:TILE] = picked
        copies = []
        for mine, (device, theirs) in enumerate(neighbours):
            copies.append(
                remote(
                    pk.at[k, mine, pl.ds(0, TILE)],
                    pk.at[k, theirs, pl.ds(TILE, TILE)],
                    p_ssem.at[k, mine],
                    p_rsem.at[k, theirs],
                    device,
                )
            )
        for copy in copies:
            copy.start()
        return copies

    def preconditioned(k, faces):
        parts = []
        for at in faces:
            here = face_rows(at)
            spread = jnp.dot(bb[here, 0 : 2 * TILE], pk[k, at], preferred_element_type=F32)
            total = t_val[here, :] + t_recv[k, here, :].astype(F32) + spread
            parts.append(total * masks[here, :])
        return parts

    def operate(k, vector):
        mapped = jnp.dot(schur[...], vector.astype(BF16), preferred_element_type=F32)
        s_send[k] = mapped.astype(BF16)
        copies = exchange(s_send.at[k], s_recv.at[k], s_ssem.at[k], s_rsem.at[k])
        finish(copies)
        return (mapped + s_recv[k].astype(F32)) * masks[...], copies

    def owned(first, second):
        total = first * second
        east_part = jnp.sum(total[face : 2 * face], axis=0, keepdims=True)
        north_part = jnp.sum(total[3 * face :], axis=0, keepdims=True)
        return east_part + north_part

    def split(value):
        high = value.astype(BF16).astype(F32)
        return high, value - high

    finish(start_copies)
    load_linv.wait()
    t_copies = [coarse_start(0, rows[...], [])]

    wait_bytes(name_plane, n_plane - 1, name_recv.at[0])
    plane_names = name_plane[...].reshape(n_plane * TILE, name_msg.shape[1]).astype(F32)
    plane_names = plane_names[:, 0:1] * 64.0 + plane_names[:, half : half + 1]
    target = lax.broadcasted_iota(jnp.int32, (1, 8 * n_z), 1)
    place = 8 * b + lax.rem(target, 8)
    wanted = jnp.where(place < cc, cc * (2 * (target // 8) + c) + place, CODE + place - cc)
    hits = jnp.where(plane_names == wanted.astype(F32), 1.0, 0.0).astype(F32)
    sel_t[...] = hits.T.astype(BF16)

    coarse_scatter(0)

    wait_bytes(name_gx, n_gx - 1, name_recv.at[1])
    gx_names = name_gx[...].reshape(n_gx * TILE, name_msg.shape[1]).astype(F32)
    gx_names = gx_names[:, 0:1] * 64.0 + gx_names[:, half : half + 1]
    wait_bytes(strip.reshape(n_gy, cr, strip_w), n_gy - 1, strip_recv)
    chunk = 256 if nc % 256 == 0 else nc // 3
    column = lax.broadcasted_iota(jnp.int32, (1, chunk), 1).astype(F32)

    def select(step, total):
        base = pl.multiple_of(step * chunk, chunk)
        hit = jnp.where(gx_names - (base * 1.0) == column, 1.0, 0.0).astype(BF16)
        return total + jnp.dot(hit, strip[pl.ds(base, chunk), :], preferred_element_type=F32)

    chosen = lax.fori_loop(
        0, nc // chunk, select, jnp.zeros((n_gx * TILE, strip_w), F32)
    )
    tsel[...] = chosen.astype(BF16).reshape(2, n_z * TILE, strip_w)
    c2[c] = tsel[c]
    c2_copy = remote(
        tsel.at[1 - c], c2.at[c], c2_send, c2_recv, {"gx": 2 * z + 1 - c, "gy": b}
    )
    c2_copy.start()

    coarse_gather(0)
    finish(bt_copies)
    bb[...] = bb[...] + bt_recv[...]
    masks[0:face, :] = jnp.broadcast_to(
        bt_recv[0:face, MASK_LANE : MASK_LANE + 1].astype(F32), (face, load_cases)
    )
    masks[2 * face : 3 * face, :] = jnp.broadcast_to(
        bt_recv[2 * face : 3 * face, MASK_LANE : MASK_LANE + 1].astype(F32),
        (face, load_cases),
    )
    c2_copy.wait_recv()
    coarse_solve(0)
    finish(t_copies[0])
    pk_copies = [coarse_finish(0)]
    finish(pk_copies[0])
    for at, part in enumerate(preconditioned(0, range(4))):
        v0[face_rows(at), :] = part

    load_schur.wait()
    first = v0[...]
    image, copies = operate(0, first)
    s_copies = [copies]
    w0[...] = image
    start = rows[...].astype(F32)
    old, curve = owned(start, first), owned(first, image)

    t_copies.append(coarse_start(1, image.astype(BF16), [*split(old), *split(curve)]))
    coarse_scatter(1)
    coarse_gather(1)
    coarse_solve(1)
    finish(t_copies[1])
    sums = sums_of(1)
    old = sums[0] + sums[1]
    curve = sums[2] + sums[3]
    step = old / curve
    pk_copies.append(coarse_finish(1))
    finish(pk_copies[1])
    for at, part in enumerate(preconditioned(1, range(4))):
        here = face_rows(at)
        v1[here, :] = part
        z1[here, :] = v0[here, :] - step * part

    second = z1[...]
    image, copies = operate(1, second)
    s_copies.append(copies)
    residual = rows[...].astype(F32) - step * w0[...]
    new = owned(residual, second)
    cross = owned(second, w0[...])
    high, low = split(owned(second, image))

    t_copies.append(coarse_start(2, image.astype(BF16), [new, high, low, cross]))
    coarse_scatter(2)
    coarse_gather(2)
    coarse_solve(2)
    finish(t_copies[2])
    sums = sums_of(2)
    new = sums[0]
    ratio = new / old
    step_two = new / (sums[1] + sums[2] + ratio * (2.0 * sums[3] + ratio * curve))
    pk_copies.append(coarse_finish(2))
    finish(pk_copies[2])
    for half_at, (at, part) in enumerate(zip((1, 3), preconditioned(2, (1, 3)))):
        here = face_rows(at)
        there = pl.ds(half_at * face, face)
        second = z1[here, :]
        direction = second + ratio * v0[here, :]
        sol_out[there, :] = step * v0[here, :] + step_two * direction
        pre_out[there, :] = second - step_two * (part + ratio * v1[here, :])

    for copy in start_copies + bt_copies + [c2_copy]:
        copy.wait_send()
    wait_bytes(name_plane, n_plane - 1, name_send.at[0])
    wait_bytes(name_gx, n_gx - 1, name_send.at[1])
    wait_bytes(strip.reshape(n_gy, cr, strip_w), n_gy - 1, strip_send)
    for k in range(SOLVES):
        for copy in t_copies[k] + pk_copies[k]:
            copy.wait_send()
        wait_bytes(g_buf.at[k], n_plane - 1, stage_send.at[k, 0])
        wait_bytes(xr.at[k], n_z - 1, stage_send.at[k, 1])
        wait_bytes(xb.at[k], n_plane - 1, stage_send.at[k, 2])
        wait_bytes(yr.at[k], n_z - 1, stage_send.at[k, 3])
    for k in range(OPS):
        for copy in s_copies[k]:
            copy.wait_send()


def shards(
    n_gx, n_gy, loads, schur, local_inv, coarse_basis, coarse_index, face_nodes, coarse_inverse
):
    owned, cases = loads.shape[2:]
    local = schur.shape[-1]
    cr, cc = coarse_inverse.shape
    nc = cr * n_gy
    n_z = n_gx // 2
    n_plane = 2 * n_gy
    strip_w = 8 * n_gy
    dma = pltpu.SemaphoreType.DMA
    vmem = pl.BlockSpec(memory_space=pltpu.VMEM)
    smem = pl.BlockSpec(memory_space=pltpu.SMEM)
    anywhere = pl.BlockSpec(memory_space=pl.ANY)
    scratch = [
        pltpu.VMEM((local, local), BF16),
        pltpu.VMEM((local, local), BF16),
        pltpu.VMEM((BT_LANES, local), F32),
        pltpu.VMEM((local, BT_LANES), BF16),
        pltpu.VMEM((local, BT_LANES), BF16),
        pltpu.VMEM((local, BT_LANES), BF16),
        pltpu.VMEM((local, cases), F32),
        pltpu.VMEM((local, cases), BF16),
        pltpu.VMEM((TILE, 128), BF16),
        pltpu.VMEM((n_plane, TILE, 128), BF16),
        pltpu.VMEM((n_gx, TILE, 128), BF16),
        pltpu.VMEM((8 * n_z, n_plane * TILE), BF16),
        pltpu.VMEM((nc, strip_w), BF16),
        pltpu.VMEM((2, n_z * TILE, strip_w), BF16),
        pltpu.VMEM((2, n_z * TILE, strip_w), BF16),
        pltpu.VMEM((local, cases), F32),
        pltpu.VMEM((SOLVES, local, cases), BF16),
        pltpu.VMEM((SOLVES, local, cases), BF16),
        pltpu.VMEM((OPS, local, cases), BF16),
        pltpu.VMEM((OPS, local, cases), BF16),
        pltpu.VMEM((SOLVES, TILE, cases), BF16),
        pltpu.VMEM((SOLVES, n_plane, TILE, cases), BF16),
        pltpu.VMEM((SOLVES, n_z, 8, cases), F32),
        pltpu.VMEM((SOLVES, n_z, 8, cases), F32),
        pltpu.VMEM((SOLVES, 8, cases), F32),
        pltpu.VMEM((SOLVES, n_plane, 8, cases), F32),
        pltpu.VMEM((SOLVES, n_z, TILE, cases), BF16),
        pltpu.VMEM((SOLVES, n_z, TILE, cases), BF16),
        pltpu.VMEM((SOLVES, 4, 2 * TILE, cases), BF16),
        pltpu.VMEM((local, cases), F32),
        pltpu.VMEM((local, cases), F32),
        pltpu.VMEM((local, cases), F32),
        pltpu.VMEM((local, cases), F32),
        dma((2,)),
        dma((8,)),
        dma((8,)),
        dma((2,)),
        dma((2,)),
        dma,
        dma,
        dma,
        dma,
        dma((SOLVES, 4)),
        dma((SOLVES, 4)),
        dma((SOLVES, 4)),
        dma((SOLVES, 4)),
        dma((OPS, 4)),
        dma((OPS, 4)),
        dma((SOLVES, 4)),
        dma((SOLVES, 4)),
    ]
    solution, precond = pl.pallas_call(
        functools.partial(kernel, n_gx, n_gy),
        out_shape=(
            jax.ShapeDtypeStruct((owned, cases), F32),
            jax.ShapeDtypeStruct((owned, cases), F32),
        ),
        in_specs=[vmem, anywhere, anywhere, vmem, smem, smem, vmem],
        out_specs=(vmem, vmem),
        scratch_shapes=scratch,
        compiler_params=pltpu.CompilerParams(
            collective_id=0, has_side_effects=True, vmem_limit_bytes=40 * 1024 * 1024
        ),
        name="bddc_cg",
    )(
        loads[0, 0],
        schur[0, 0],
        local_inv[0, 0],
        coarse_basis[0, 0],
        coarse_index[0, 0],
        face_nodes[0, 0],
        coarse_inverse,
    )
    return solution[None, None], precond[None, None]


def solution(mesh):
    placed = (
        P("gx", "gy", None, None),
        P("gx", "gy", None, None),
        P("gx", "gy", None, None),
        P("gx", "gy", None, None),
        P("gx", "gy", None),
        P("gx", "gy", None),
        P("gy", "gx"),
    )
    return jax.shard_map(
        functools.partial(shards, mesh.shape["gx"], mesh.shape["gy"]),
        mesh=mesh,
        in_specs=placed,
        out_specs=(P("gx", "gy", None, None), P("gx", "gy", None, None)),
        check_vma=False,
    )
```

```python
import functools
import math
import jax
import jax.numpy as jnp
from jax import lax
from jax.experimental import pallas as pl
from jax.experimental.pallas import tpu as pltpu
from jax.sharding import PartitionSpec as P

MESH = pl.DeviceIdType.MESH
F32 = jnp.float32
BF16 = jnp.bfloat16
TILE = 16
CODE = 4096
MASK_LANE = 64
BT_LANES = 128
SOLVES = 3
OPS = 2


def kernel(
    n_gx,
    n_gy,
    loads,
    schur_hbm,
    linv_hbm,
    basis,
    index,
    nodes,
    cinv,
    sol_out,
    pre_out,
    schur,
    linv,
    bpad,
    bt_send,
    bt_recv,
    bb,
    masks,
    rows,
    name_msg,
    name_plane,
    name_gx,
    sel_t,
    strip,
    tsel,
    c2,
    c_own,
    name_cols,
    name_lane_msg,
    tau_strip,
    tau_low,
    c_nat,
    c_line,
    c_full,
    t_val,
    t_send,
    t_recv,
    s_send,
    s_recv,
    g_msg,
    g_buf,
    xs,
    xr,
    x_msg,
    xb,
    ys,
    yr,
    pk,
    v0,
    v1,
    z1,
    w0,
    load_sem,
    face_send,
    face_recv,
    name_send,
    name_recv,
    strip_send,
    strip_recv,
    c2_send,
    c2_recv,
    perm_send,
    perm_recv,
    stage_send,
    stage_recv,
    t_ssem,
    t_rsem,
    s_ssem,
    s_rsem,
    p_ssem,
    p_rsem,
):
    a = lax.axis_index("gx")
    b = lax.axis_index("gy")
    n_z = n_gx // 2
    n_plane = 2 * n_gy
    z = a // 2
    c = lax.rem(a, 2)
    slot = c * n_gy + b
    local = schur.shape[0]
    face = local // 4
    nodes_per = face // 3
    cr, cc = cinv.shape
    strip_w = 8 * n_gy
    nc = cr * n_gy
    load_cases = loads.shape[1]

    side = math.isqrt(n_gy)

    def far_first(step, extent):
        half = (step + 1) // 2
        return extent // 2 + jnp.where(lax.rem(step, 2) == 1, -half, half)

    def plane_peer(step, other_core):
        y = lax.rem(b // side + far_first(step // side, side), side)
        x = lax.rem(lax.rem(b, side) + far_first(lax.rem(step, side), side), side)
        return {"gx": 2 * z + lax.rem(c + other_core, 2), "gy": y * side + x}

    def line_peer(step):
        return lax.rem(z + far_first(step, n_z), n_z)

    def signal(device):
        pl.semaphore_signal(barrier, inc=1, device_id=device, device_id_type=MESH)

    barrier = pltpu.get_barrier_semaphore()

    @pl.loop(0, n_z - 1)
    def _(step):
        other = line_peer(step)
        signal({"gx": 2 * other, "gy": b})
        signal({"gx": 2 * other + 1, "gy": b})

    @pl.loop(0, n_gy - 1)
    def _(step):
        signal(plane_peer(step, 0))
        signal(plane_peer(step, 1))

    signal(plane_peer(n_gy - 1, 1))

    load_linv = pltpu.make_async_copy(linv_hbm, linv, load_sem.at[0])
    load_schur = pltpu.make_async_copy(schur_hbm, schur, load_sem.at[1])
    load_linv.start()
    load_schur.start()

    def remote(src, dst, send, recv, device):
        return pltpu.make_async_remote_copy(
            src_ref=src,
            dst_ref=dst,
            send_sem=send,
            recv_sem=recv,
            device_id=device,
            device_id_type=MESH,
        )

    def plane_send(src, dst, send, recv):
        @pl.loop(0, n_gy - 1)
        def _(step):
            remote(src, dst.at[slot], send, recv, plane_peer(step, 0)).start()
            remote(src, dst.at[slot], send, recv, plane_peer(step, 1)).start()

        remote(src, dst.at[slot], send, recv, plane_peer(n_gy - 1, 1)).start()

    def z_send(src, dst, send, recv):
        @pl.loop(0, n_z - 1)
        def _(step):
            other = line_peer(step)
            remote(
                src.at[other], dst.at[z], send, recv, {"gx": 2 * other + c, "gy": b}
            ).start()

    def wait_bytes(buf, count, sem):
        part = buf.at[pl.ds(0, count)]
        pltpu.make_async_copy(part, part, sem).wait()

    west = {"gx": lax.rem(a + n_gx - 1, n_gx), "gy": b}
    east = {"gx": lax.rem(a + 1, n_gx), "gy": b}
    south = {"gx": a, "gy": lax.rem(b + n_gy - 1, n_gy)}
    north = {"gx": a, "gy": lax.rem(b + 1, n_gy)}
    neighbours = ((west, 1), (east, 0), (south, 3), (north, 2))

    def face_rows(which):
        return pl.ds(which * face, face)

    def exchange(src, dst, send, recv):
        copies = []
        for mine, (device, theirs) in enumerate(neighbours):
            copies.append(
                remote(
                    src.at[face_rows(mine)],
                    dst.at[face_rows(theirs)],
                    send.at[mine],
                    recv.at[theirs],
                    device,
                )
            )
        for copy in copies:
            copy.start()
        return copies

    def finish(copies):
        for copy in copies:
            copy.wait_recv()

    lane = lax.broadcasted_iota(jnp.int32, (1, local), 1)
    which = lane // face
    node = lax.rem(lax.rem(lane, face), nodes_per)
    alive_east = (which == 1) & (node < nodes[0]) & (a < n_gx - 1)
    alive_north = (which == 3) & (node < nodes[1]) & (b < n_gy - 1)
    mask_row = jnp.where(alive_east | alive_north, 1.0, 0.0).astype(F32)
    basis_wide = basis[...].astype(F32)
    n_primal = basis_wide.shape[0]

    bpad[...] = jnp.zeros_like(bpad)
    bpad[TILE : TILE + n_primal, :] = basis_wide
    bpad[MASK_LANE : MASK_LANE + 1, :] = mask_row
    flipped = bpad[...].T
    bt_send[...] = flipped.astype(BF16)
    masks[...] = jnp.broadcast_to(flipped[:, MASK_LANE : MASK_LANE + 1], masks.shape)
    bpad[...] = jnp.zeros_like(bpad)
    bpad[0:n_primal, :] = basis_wide
    bb[...] = bpad[...].T.astype(BF16)
    basis16 = bpad[0:TILE, :].astype(BF16)

    rows[face : 2 * face, :] = (
        loads[0:face, :].astype(F32) * masks[face : 2 * face, :]
    ).astype(BF16)
    rows[3 * face :, :] = (
        loads[face:, :].astype(F32) * masks[3 * face :, :]
    ).astype(BF16)

    name_row = lax.broadcasted_iota(jnp.int32, name_msg.shape, 0)
    name_lane = lax.broadcasted_iota(jnp.int32, name_msg.shape, 1)
    names = CODE + name_row - n_primal
    for j in range(n_primal):
        names = jnp.where(name_row == j, index[j], names)
    half = name_msg.shape[1] // 2
    name_msg[...] = (
        jnp.where(name_lane < half, names // 64, lax.rem(names, 64)).astype(F32).astype(BF16)
    )
    name_plane[slot] = name_msg[...]
    name_gx[c * n_z + z] = name_msg[...]

    my_strip = strip.at[pl.ds(pl.multiple_of(b * cr, 8), cr)]
    wide = jnp.concatenate(
        [cinv[...].astype(BF16), jnp.zeros((cr, strip_w - cc), BF16)], axis=1
    )
    strip[pl.ds(pl.multiple_of(b * cr, 8), cr), :] = wide

    pl.semaphore_wait(barrier, n_plane - 1 + n_gx - 2)

    start_copies = []
    for mine, (device, theirs) in ((1, (east, 0)), (3, (north, 2))):
        copy = remote(
            rows.at[face_rows(mine)],
            rows.at[face_rows(theirs)],
            face_send.at[mine],
            face_recv.at[theirs],
            device,
        )
        copy.start()
        start_copies.append(copy)

    plane_send(name_msg, name_plane, name_send.at[0], name_recv.at[0])

    @pl.loop(1, n_gx)
    def _(k):
        other = lax.rem(a + k, n_gx)
        remote(
            name_msg,
            name_gx.at[c * n_z + z],
            name_send.at[1],
            name_recv.at[1],
            {"gx": other, "gy": b},
        ).start()

    @pl.loop(1, n_gy)
    def _(k):
        other = lax.rem(b + k, n_gy)
        remote(my_strip, my_strip, strip_send, strip_recv, {"gx": a, "gy": other}).start()

    bt_copies = exchange(bt_send, bt_recv, face_send.at[pl.ds(4, 4)], face_recv.at[pl.ds(4, 4)])

    def coarse_start(k, local_rows, sums):
        primal = jnp.dot(basis16, local_rows, preferred_element_type=F32)
        for j, value in enumerate(sums):
            at = lax.broadcasted_iota(jnp.int32, primal.shape, 0) == n_primal + j
            primal = jnp.where(at, value, primal)
        message = primal.astype(BF16)
        g_msg[k] = message
        g_buf[k, slot] = message
        plane_send(g_msg.at[k], g_buf.at[k], stage_send.at[k, 0], stage_recv.at[k, 0])
        t_val[...] = jnp.dot(linv[...], local_rows, preferred_element_type=F32)
        t_send[k] = t_val[...].astype(BF16)
        return exchange(t_send.at[k], t_recv.at[k], t_ssem.at[k], t_rsem.at[k])

    def coarse_scatter(k):
        wait_bytes(g_buf.at[k], n_plane - 1, stage_recv.at[k, 0])
        gathered = g_buf[k].reshape(n_plane * TILE, load_cases)
        part = jnp.dot(sel_t[...], gathered, preferred_element_type=F32)
        part = part.reshape(n_z, 8, load_cases)
        xs[k] = part
        xr[k, z] = xs[k, z]
        z_send(xs.at[k], xr.at[k], stage_send.at[k, 1], stage_recv.at[k, 1])

    def coarse_gather(k):
        wait_bytes(xr.at[k], n_z - 1, stage_recv.at[k, 1])
        mine = jnp.sum(xr[k], axis=0)
        x_msg[k] = mine
        xb[k, slot] = mine
        plane_send(x_msg.at[k], xb.at[k], stage_send.at[k, 2], stage_recv.at[k, 2])

    def coarse_solve(k):
        wait_bytes(xb.at[k], n_plane - 1, stage_recv.at[k, 2])
        low = xb[k, 0:n_gy].reshape(strip_w, load_cases).astype(BF16)
        high = xb[k, n_gy:].reshape(strip_w, load_cases).astype(BF16)
        part = jnp.dot(c2[0], low, preferred_element_type=F32) + jnp.dot(
            c2[1], high, preferred_element_type=F32
        )
        ys[k] = part.astype(BF16).reshape(n_z, TILE, load_cases)
        yr[k, z] = ys[k, z]
        z_send(ys.at[k], yr.at[k], stage_send.at[k, 3], stage_recv.at[k, 3])

    def coarse_direct(k):
        wait_bytes(g_buf.at[k], n_plane - 1, stage_recv.at[k, 0])
        gathered = g_buf[k].reshape(n_plane * TILE, load_cases)
        part = jnp.dot(c_full[...], gathered, preferred_element_type=F32)
        at = lax.rem(lax.broadcasted_iota(jnp.int32, part.shape, 0), TILE)
        rest = part - part.astype(BF16).astype(F32)
        part = jnp.where((at == n_primal + 1) | (at == n_primal + 3), rest, part)
        ys[k] = part.astype(BF16).reshape(n_z, TILE, load_cases)
        yr[k, z] = ys[k, z]
        z_send(ys.at[k], yr.at[k], stage_send.at[k, 3], stage_recv.at[k, 3])

    def coarse_finish(k):
        wait_bytes(yr.at[k], n_z - 1, stage_recv.at[k, 3])
        total = jnp.sum(yr[k].astype(F32), axis=0)
        picked = total.astype(BF16)
        for at in range(4):
            pk[k, at, 0:TILE] = picked
        copies = []
        for mine, (device, theirs) in enumerate(neighbours):
            copies.append(
                remote(
                    pk.at[k, mine, pl.ds(0, TILE)],
                    pk.at[k, theirs, pl.ds(TILE, TILE)],
                    p_ssem.at[k, mine],
                    p_rsem.at[k, theirs],
                    device,
                )
            )
        for copy in copies:
            copy.start()
        first = total[n_primal : n_primal + 1] + total[n_primal + 1 : n_primal + 2]
        second = total[n_primal + 2 : n_primal + 3] + total[n_primal + 3 : n_primal + 4]
        return copies, first, second

    def preconditioned(k, faces):
        parts = []
        for at in faces:
            here = face_rows(at)
            spread = jnp.dot(bb[here, 0 : 2 * TILE], pk[k, at], preferred_element_type=F32)
            total = t_val[here, :] + t_recv[k, here, :].astype(F32) + spread
            parts.append(total * masks[here, :])
        return parts

    def operate(k, vector):
        mapped = jnp.dot(schur[...], vector.astype(BF16), preferred_element_type=F32)
        s_send[k] = mapped.astype(BF16)
        copies = exchange(s_send.at[k], s_recv.at[k], s_ssem.at[k], s_rsem.at[k])
        finish(copies)
        return (mapped + s_recv[k].astype(F32)) * masks[...], copies

    def owned(first, second):
        total = first * second
        east_part = jnp.sum(total[face : 2 * face], axis=0, keepdims=True)
        north_part = jnp.sum(total[3 * face :], axis=0, keepdims=True)
        return east_part + north_part

    def split(value):
        high = value.astype(BF16).astype(F32)
        return high, value - high

    finish(start_copies)
    load_linv.wait()
    t_copies = [coarse_start(0, rows[...], [])]

    wait_bytes(name_plane, n_plane - 1, name_recv.at[0])
    plane_names = name_plane[...].reshape(n_plane * TILE, name_msg.shape[1]).astype(F32)
    plane_names = plane_names[:, 0:1] * 64.0 + plane_names[:, half : half + 1]
    target = lax.broadcasted_iota(jnp.int32, (1, 8 * n_z), 1)
    place = 8 * b + lax.rem(target, 8)
    wanted = jnp.where(place < cc, cc * (2 * (target // 8) + c) + place, CODE + place - cc)
    hits = jnp.where(plane_names == wanted.astype(F32), 1.0, 0.0).astype(F32)
    sel_t[...] = hits.T.astype(BF16)

    coarse_scatter(0)

    wait_bytes(name_gx, n_gx - 1, name_recv.at[1])
    gx_names = name_gx[...].reshape(n_gx * TILE, name_msg.shape[1]).astype(F32)
    gx_names = gx_names[:, 0:1] * 64.0 + gx_names[:, half : half + 1]

    width = c_nat.shape[2]
    face_cols = 3 * n_gy
    lanes = lax.broadcasted_iota(jnp.int32, (TILE, width), 1)
    prim = lax.broadcasted_iota(jnp.int32, (TILE, width), 0)
    within = 3 * b + lax.rem(prim, 3)
    low_face = jnp.where(prim < 3, 0, jnp.where(prim < 6, 1, 3))
    high_face = jnp.where(prim < 6, 2, 4)
    owned_prim = ((prim >= 3) & (prim < 6)) | ((prim >= 9) & (prim < 12))
    low_hit = (lanes == low_face * face_cols + within) & (owned_prim | (prim < 3))
    high_hit = (lanes == high_face * face_cols + within) & owned_prim
    spread_names = jnp.broadcast_to(gx_names, (n_gx * TILE, width)).reshape(
        n_gx, TILE, width
    )
    lane_names = jnp.sum(
        jnp.where(low_hit[None], spread_names[:n_z], 0.0)
        + jnp.where(high_hit[None], spread_names[n_z:], 0.0),
        axis=1,
    )
    name_lane_msg[...] = lane_names
    name_cols[b] = lane_names

    @pl.loop(1, n_gy)
    def _(k):
        remote(
            name_lane_msg,
            name_cols.at[b],
            perm_send.at[0],
            perm_recv.at[0],
            {"gx": a, "gy": lax.rem(b + k, n_gy)},
        ).start()

    wait_bytes(strip.reshape(n_gy, cr, strip_w), n_gy - 1, strip_recv)
    chunk = 256 if nc % 256 == 0 else nc // 3
    column = lax.broadcasted_iota(jnp.int32, (1, chunk), 1).astype(F32)

    def select(step, total):
        base = pl.multiple_of(step * chunk, chunk)
        hit = jnp.where(gx_names - (base * 1.0) == column, 1.0, 0.0).astype(BF16)
        return total + jnp.dot(hit, strip[pl.ds(base, chunk), :], preferred_element_type=F32)

    chosen = lax.fori_loop(
        0, nc // chunk, select, jnp.zeros((n_gx * TILE, strip_w), F32)
    )
    tsel[...] = chosen.astype(BF16).reshape(2, n_z * TILE, strip_w)
    c2[c] = tsel[c]
    c2_copy = remote(
        tsel.at[1 - c], c2.at[c], c2_send, c2_recv, {"gx": 2 * z + 1 - c, "gy": b}
    )
    c2_copy.start()
    c_own[a] = tsel[c, pl.ds(pl.multiple_of(z * TILE, TILE), TILE)]

    def send_rows(core, other):
        remote(
            tsel.at[core, pl.ds(pl.multiple_of(other * TILE, TILE), TILE)],
            c_own.at[a],
            perm_send.at[1],
            perm_recv.at[1],
            {"gx": 2 * other + core, "gy": b},
        ).start()

    @pl.loop(0, n_z - 1)
    def _(step):
        other = line_peer(step)
        send_rows(0, other)
        send_rows(1, other)

    send_rows(1 - c, z)

    coarse_gather(0)
    finish(bt_copies)
    bb[...] = bb[...] + bt_recv[...]
    masks[0:face, :] = jnp.broadcast_to(
        bt_recv[0:face, MASK_LANE : MASK_LANE + 1].astype(F32), (face, load_cases)
    )
    masks[2 * face : 3 * face, :] = jnp.broadcast_to(
        bt_recv[2 * face : 3 * face, MASK_LANE : MASK_LANE + 1].astype(F32),
        (face, load_cases),
    )
    c2_copy.wait_recv()
    coarse_solve(0)

    wait_bytes(name_cols, n_gy - 1, perm_recv.at[0])
    col_names = jnp.sum(name_cols[...], axis=0)
    used = lax.broadcasted_iota(jnp.int32, col_names.shape, 1) < 5 * face_cols
    col_strip = ((col_names + 0.5) * (1.0 / cc)).astype(jnp.int32)
    col_low = col_names.astype(jnp.int32) - cc * col_strip
    tau_strip[...] = col_strip
    tau_low[...] = jnp.where(used, col_low, -1)
    wait_bytes(c_own, n_gx - 1, perm_recv.at[1])
    inner = lax.broadcasted_iota(jnp.int32, (strip_w, 1), 0)
    strips = lax.broadcasted_iota(jnp.int32, (n_gx, 1, 1), 0)

    @pl.loop(0, n_z)
    def _(step):
        picks = jnp.where(inner == tau_low[pl.ds(step, 1), :], 1.0, 0.0).astype(BF16)
        mine = c_own[...].reshape(n_gx * TILE, strip_w)
        wide_rows = jnp.dot(mine, picks, preferred_element_type=F32)
        wide_rows = wide_rows.reshape(n_gx, TILE, width)
        hit = strips == tau_strip[pl.ds(step, 1), :][None]
        c_nat[step] = jnp.sum(jnp.where(hit, wide_rows, 0.0), axis=0).astype(BF16)

    c_line[z] = c_nat[z]
    z_send(c_nat, c_line, perm_send.at[2], perm_recv.at[2])

    finish(t_copies[0])
    pk_copies = [coarse_finish(0)[0]]
    finish(pk_copies[0])
    for at, part in enumerate(preconditioned(0, range(4))):
        v0[face_rows(at), :] = part

    load_schur.wait()
    first = v0[...]
    image, copies = operate(0, first)
    s_copies = [copies]
    w0[...] = image
    start = rows[...].astype(F32)
    old, curve = owned(start, first), owned(first, image)

    t_copies.append(coarse_start(1, image.astype(BF16), [*split(old), *split(curve)]))

    wait_bytes(c_line, n_z - 1, perm_recv.at[2])
    at = lax.broadcasted_iota(jnp.int32, (1, n_plane * TILE), 1)
    at_slot, at_prim = at // TILE, lax.rem(at, TILE)
    at_core, at_b = at_slot // n_gy, lax.rem(at_slot, n_gy)
    at_face = jnp.where(
        at_prim < 3, at_core, jnp.where(at_prim < 6, 1 + at_core, 3 + at_core)
    )
    at_b = jnp.where((at_prim >= 6) & (at_prim < 9), lax.rem(at_b + n_gy - 1, n_gy), at_b)
    at_col = jnp.where(
        at_prim < 12, at_face * face_cols + 3 * at_b + lax.rem(at_prim, 3), -1
    )
    place = jnp.where(
        lax.broadcasted_iota(jnp.int32, (width, 1), 0) == at_col, 1.0, 0.0
    ).astype(BF16)
    block = jnp.dot(
        c_line[...].reshape(n_z * TILE, width), place, preferred_element_type=F32
    )
    row_prim = lax.rem(lax.broadcasted_iota(jnp.int32, (n_z * TILE, 1), 0), TILE)
    adds = (row_prim >= 12) & (at_prim >= 12) & (row_prim // 2 == at_prim // 2)
    c_full[...] = jnp.where(adds, 1.0, block).astype(BF16)

    coarse_direct(1)
    finish(t_copies[1])
    copies, old, curve = coarse_finish(1)
    step = old / curve
    pk_copies.append(copies)
    finish(pk_copies[1])
    for at, part in enumerate(preconditioned(1, range(4))):
        here = face_rows(at)
        v1[here, :] = part
        z1[here, :] = v0[here, :] - step * part

    second = z1[...]
    image, copies = operate(1, second)
    s_copies.append(copies)
    residual = rows[...].astype(F32) - step * w0[...]
    new, second_curve = owned(residual, second), owned(second, image)

    t_copies.append(coarse_start(2, image.astype(BF16), [*split(new), *split(second_curve)]))
    coarse_direct(2)
    finish(t_copies[2])
    copies, new, second_curve = coarse_finish(2)
    ratio = new / old
    step_two = new / (second_curve - ratio * ratio * curve)
    pk_copies.append(copies)
    finish(pk_copies[2])
    for half_at, (at, part) in enumerate(zip((1, 3), preconditioned(2, (1, 3)))):
        here = face_rows(at)
        there = pl.ds(half_at * face, face)
        second = z1[here, :]
        direction = second + ratio * v0[here, :]
        sol_out[there, :] = step * v0[here, :] + step_two * direction
        pre_out[there, :] = second - step_two * (part + ratio * v1[here, :])

    for copy in start_copies + bt_copies + [c2_copy]:
        copy.wait_send()
    wait_bytes(name_plane, n_plane - 1, name_send.at[0])
    wait_bytes(name_gx, n_gx - 1, name_send.at[1])
    wait_bytes(strip.reshape(n_gy, cr, strip_w), n_gy - 1, strip_send)
    wait_bytes(name_cols, n_gy - 1, perm_send.at[0])
    wait_bytes(c_own, n_gx - 1, perm_send.at[1])
    wait_bytes(c_line, n_z - 1, perm_send.at[2])
    wait_bytes(xr.at[0], n_z - 1, stage_send.at[0, 1])
    wait_bytes(xb.at[0], n_plane - 1, stage_send.at[0, 2])
    for k in range(SOLVES):
        for copy in t_copies[k] + pk_copies[k]:
            copy.wait_send()
        wait_bytes(g_buf.at[k], n_plane - 1, stage_send.at[k, 0])
        wait_bytes(yr.at[k], n_z - 1, stage_send.at[k, 3])
    for k in range(OPS):
        for copy in s_copies[k]:
            copy.wait_send()


def shards(
    n_gx, n_gy, loads, schur, local_inv, coarse_basis, coarse_index, face_nodes, coarse_inverse
):
    owned, cases = loads.shape[2:]
    local = schur.shape[-1]
    cr, cc = coarse_inverse.shape
    nc = cr * n_gy
    n_z = n_gx // 2
    n_plane = 2 * n_gy
    strip_w = 8 * n_gy
    dma = pltpu.SemaphoreType.DMA
    vmem = pl.BlockSpec(memory_space=pltpu.VMEM)
    smem = pl.BlockSpec(memory_space=pltpu.SMEM)
    anywhere = pl.BlockSpec(memory_space=pl.ANY)
    scratch = [
        pltpu.VMEM((local, local), BF16),
        pltpu.VMEM((local, local), BF16),
        pltpu.VMEM((BT_LANES, local), F32),
        pltpu.VMEM((local, BT_LANES), BF16),
        pltpu.VMEM((local, BT_LANES), BF16),
        pltpu.VMEM((local, BT_LANES), BF16),
        pltpu.VMEM((local, cases), F32),
        pltpu.VMEM((local, cases), BF16),
        pltpu.VMEM((TILE, 128), BF16),
        pltpu.VMEM((n_plane, TILE, 128), BF16),
        pltpu.VMEM((n_gx, TILE, 128), BF16),
        pltpu.VMEM((8 * n_z, n_plane * TILE), BF16),
        pltpu.VMEM((nc, strip_w), BF16),
        pltpu.VMEM((2, n_z * TILE, strip_w), BF16),
        pltpu.VMEM((2, n_z * TILE, strip_w), BF16),
        pltpu.VMEM((n_gx, TILE, strip_w), BF16),
        pltpu.VMEM((n_gy, n_z, 16 * n_gy), F32),
        pltpu.VMEM((n_z, 16 * n_gy), F32),
        pltpu.VMEM((n_z, 16 * n_gy), jnp.int32),
        pltpu.VMEM((n_z, 16 * n_gy), jnp.int32),
        pltpu.VMEM((n_z, TILE, 16 * n_gy), BF16),
        pltpu.VMEM((n_z, TILE, 16 * n_gy), BF16),
        pltpu.VMEM((n_z * TILE, n_plane * TILE), BF16),
        pltpu.VMEM((local, cases), F32),
        pltpu.VMEM((SOLVES, local, cases), BF16),
        pltpu.VMEM((SOLVES, local, cases), BF16),
        pltpu.VMEM((OPS, local, cases), BF16),
        pltpu.VMEM((OPS, local, cases), BF16),
        pltpu.VMEM((SOLVES, TILE, cases), BF16),
        pltpu.VMEM((SOLVES, n_plane, TILE, cases), BF16),
        pltpu.VMEM((SOLVES, n_z, 8, cases), F32),
        pltpu.VMEM((SOLVES, n_z, 8, cases), F32),
        pltpu.VMEM((SOLVES, 8, cases), F32),
        pltpu.VMEM((SOLVES, n_plane, 8, cases), F32),
        pltpu.VMEM((SOLVES, n_z, TILE, cases), BF16),
        pltpu.VMEM((SOLVES, n_z, TILE, cases), BF16),
        pltpu.VMEM((SOLVES, 4, 2 * TILE, cases), BF16),
        pltpu.VMEM((local, cases), F32),
        pltpu.VMEM((local, cases), F32),
        pltpu.VMEM((local, cases), F32),
        pltpu.VMEM((local, cases), F32),
        dma((2,)),
        dma((8,)),
        dma((8,)),
        dma((2,)),
        dma((2,)),
        dma,
        dma,
        dma,
        dma,
        dma((3,)),
        dma((3,)),
        dma((SOLVES, 4)),
        dma((SOLVES, 4)),
        dma((SOLVES, 4)),
        dma((SOLVES, 4)),
        dma((OPS, 4)),
        dma((OPS, 4)),
        dma((SOLVES, 4)),
        dma((SOLVES, 4)),
    ]
    solution, precond = pl.pallas_call(
        functools.partial(kernel, n_gx, n_gy),
        out_shape=(
            jax.ShapeDtypeStruct((owned, cases), F32),
            jax.ShapeDtypeStruct((owned, cases), F32),
        ),
        in_specs=[vmem, anywhere, anywhere, vmem, smem, smem, vmem],
        out_specs=(vmem, vmem),
        scratch_shapes=scratch,
        compiler_params=pltpu.CompilerParams(
            collective_id=0, has_side_effects=True, vmem_limit_bytes=60 * 1024 * 1024
        ),
        name="bddc_cg",
    )(
        loads[0, 0],
        schur[0, 0],
        local_inv[0, 0],
        coarse_basis[0, 0],
        coarse_index[0, 0],
        face_nodes[0, 0],
        coarse_inverse,
    )
    return solution[None, None], precond[None, None]


def solution(mesh):
    placed = (
        P("gx", "gy", None, None),
        P("gx", "gy", None, None),
        P("gx", "gy", None, None),
        P("gx", "gy", None, None),
        P("gx", "gy", None),
        P("gx", "gy", None),
        P("gy", "gx"),
    )
    return jax.shard_map(
        functools.partial(shards, mesh.shape["gx"], mesh.shape["gy"]),
        mesh=mesh,
        in_specs=placed,
        out_specs=(P("gx", "gy", None, None), P("gx", "gy", None, None)),
        check_vma=False,
    )
```

```python
import functools
import math
import jax
import jax.numpy as jnp
from jax import lax
from jax.experimental import pallas as pl
from jax.experimental.pallas import tpu as pltpu
from jax.sharding import PartitionSpec as P

MESH = pl.DeviceIdType.MESH
F32 = jnp.float32
BF16 = jnp.bfloat16
TILE = 16
CODE = 4096
MASK_LANE = 64
BT_LANES = 128
SOLVES = 3
OPS = 2
SLOT_LANES = 256
OFFSETS = (
    (-1, 0),
    (1, 0),
    (0, -1),
    (0, 1),
    (-2, 0),
    (2, 0),
    (0, -2),
    (0, 2),
    (-1, -1),
    (-1, 1),
    (1, -1),
    (1, 1),
)
DIAGONALS = OFFSETS[8:]
SEEN = ((1, 5, 0, 9, 10), (2, 0, 6, 11, 12), (3, 9, 11, 7, 0), (4, 10, 12, 0, 8))


def kernel(
    n_gx,
    n_gy,
    loads,
    schur_hbm,
    linv_hbm,
    basis,
    index,
    nodes,
    cinv,
    sol_out,
    pre_out,
    schur,
    linv,
    bpad,
    bt_send,
    bt_recv,
    bb,
    masks,
    rows,
    name_msg,
    name_plane,
    name_gx,
    sel_t,
    strip,
    tsel,
    c2,
    c_own,
    name_cols,
    name_lane_msg,
    tau_strip,
    tau_low,
    c_nat,
    c_line,
    c_full,
    t_val,
    t_recv,
    t_hat,
    s_val,
    s_recv,
    s_hat,
    sg_send,
    sg_recv,
    g_mat,
    h_mat,
    g_msg,
    g_buf,
    xs,
    xr,
    x_msg,
    xb,
    ys,
    yr,
    pk,
    v0,
    v1,
    z1,
    w0,
    load_sem,
    face_send,
    face_recv,
    name_send,
    name_recv,
    strip_send,
    strip_recv,
    c2_send,
    c2_recv,
    perm_send,
    perm_recv,
    stage_send,
    stage_recv,
    t_ssem,
    t_rsem,
    s_ssem,
    s_rsem,
    sg_ssem,
    sg_rsem,
    p_ssem,
    p_rsem,
):
    a = lax.axis_index("gx")
    b = lax.axis_index("gy")
    n_z = n_gx // 2
    n_plane = 2 * n_gy
    z = a // 2
    c = lax.rem(a, 2)
    slot = c * n_gy + b
    local = schur.shape[0]
    face = local // 4
    nodes_per = face // 3
    cr, cc = cinv.shape
    strip_w = 8 * n_gy
    nc = cr * n_gy
    load_cases = loads.shape[1]

    side = math.isqrt(n_gy)

    def far_first(step, extent):
        half = (step + 1) // 2
        return extent // 2 + jnp.where(lax.rem(step, 2) == 1, -half, half)

    def plane_peer(step, other_core):
        y = lax.rem(b // side + far_first(step // side, side), side)
        x = lax.rem(lax.rem(b, side) + far_first(lax.rem(step, side), side), side)
        return {"gx": 2 * z + lax.rem(c + other_core, 2), "gy": y * side + x}

    def line_peer(step):
        return lax.rem(z + far_first(step, n_z), n_z)

    def signal(device):
        pl.semaphore_signal(barrier, inc=1, device_id=device, device_id_type=MESH)

    barrier = pltpu.get_barrier_semaphore()
    pk[...] = jnp.zeros_like(pk)

    @pl.loop(0, n_z - 1)
    def _(step):
        other = line_peer(step)
        signal({"gx": 2 * other, "gy": b})
        signal({"gx": 2 * other + 1, "gy": b})

    @pl.loop(0, n_gy - 1)
    def _(step):
        signal(plane_peer(step, 0))
        signal(plane_peer(step, 1))

    signal(plane_peer(n_gy - 1, 1))

    def grid_peer(offset):
        return {
            "gx": lax.rem(a + offset[0] + n_gx, n_gx),
            "gy": lax.rem(b + offset[1] + n_gy, n_gy),
        }

    for offset in DIAGONALS:
        signal(grid_peer(offset))

    load_linv = pltpu.make_async_copy(linv_hbm, linv, load_sem.at[0])
    load_schur = pltpu.make_async_copy(schur_hbm, schur, load_sem.at[1])
    load_linv.start()
    load_schur.start()

    def remote(src, dst, send, recv, device):
        return pltpu.make_async_remote_copy(
            src_ref=src,
            dst_ref=dst,
            send_sem=send,
            recv_sem=recv,
            device_id=device,
            device_id_type=MESH,
        )

    def plane_send(src, dst, send, recv):
        @pl.loop(0, n_gy - 1)
        def _(step):
            remote(src, dst.at[slot], send, recv, plane_peer(step, 0)).start()
            remote(src, dst.at[slot], send, recv, plane_peer(step, 1)).start()

        remote(src, dst.at[slot], send, recv, plane_peer(n_gy - 1, 1)).start()

    def z_send(src, dst, send, recv):
        @pl.loop(0, n_z - 1)
        def _(step):
            other = line_peer(step)
            remote(
                src.at[other], dst.at[z], send, recv, {"gx": 2 * other + c, "gy": b}
            ).start()

    def wait_bytes(buf, count, sem):
        part = buf.at[pl.ds(0, count)]
        pltpu.make_async_copy(part, part, sem).wait()

    west = {"gx": lax.rem(a + n_gx - 1, n_gx), "gy": b}
    east = {"gx": lax.rem(a + 1, n_gx), "gy": b}
    south = {"gx": a, "gy": lax.rem(b + n_gy - 1, n_gy)}
    north = {"gx": a, "gy": lax.rem(b + 1, n_gy)}
    neighbours = ((west, 1), (east, 0), (south, 3), (north, 2))

    def face_rows(which):
        return pl.ds(which * face, face)

    def exchange(src, dst, send, recv):
        copies = []
        for mine, (device, theirs) in enumerate(neighbours):
            copies.append(
                remote(
                    src.at[face_rows(mine)],
                    dst.at[face_rows(theirs)],
                    send.at[mine],
                    recv.at[theirs],
                    device,
                )
            )
        for copy in copies:
            copy.start()
        return copies

    def finish(copies):
        for copy in copies:
            copy.wait_recv()

    lane = lax.broadcasted_iota(jnp.int32, (1, local), 1)
    which = lane // face
    node = lax.rem(lax.rem(lane, face), nodes_per)
    alive_east = (which == 1) & (node < nodes[0]) & (a < n_gx - 1)
    alive_north = (which == 3) & (node < nodes[1]) & (b < n_gy - 1)
    mask_row = jnp.where(alive_east | alive_north, 1.0, 0.0).astype(F32)
    basis_wide = basis[...].astype(F32)
    n_primal = basis_wide.shape[0]

    bpad[...] = jnp.zeros_like(bpad)
    bpad[TILE : TILE + n_primal, :] = basis_wide
    bpad[MASK_LANE : MASK_LANE + 1, :] = mask_row
    flipped = bpad[...].T
    bt_send[...] = flipped.astype(BF16)
    masks[...] = jnp.broadcast_to(flipped[:, MASK_LANE : MASK_LANE + 1], masks.shape)
    bpad[...] = jnp.zeros_like(bpad)
    bpad[0:n_primal, :] = basis_wide
    bb[...] = bpad[...].T.astype(BF16)
    basis16 = bpad[0:TILE, :].astype(BF16)

    rows[face : 2 * face, :] = (
        loads[0:face, :].astype(F32) * masks[face : 2 * face, :]
    ).astype(BF16)
    rows[3 * face :, :] = (
        loads[face:, :].astype(F32) * masks[3 * face :, :]
    ).astype(BF16)

    name_row = lax.broadcasted_iota(jnp.int32, name_msg.shape, 0)
    name_lane = lax.broadcasted_iota(jnp.int32, name_msg.shape, 1)
    names = CODE + name_row - n_primal
    for j in range(n_primal):
        names = jnp.where(name_row == j, index[j], names)
    half = name_msg.shape[1] // 2
    name_msg[...] = (
        jnp.where(name_lane < half, names // 64, lax.rem(names, 64)).astype(F32).astype(BF16)
    )
    name_plane[slot] = name_msg[...]
    name_gx[c * n_z + z] = name_msg[...]

    my_strip = strip.at[pl.ds(pl.multiple_of(b * cr, 8), cr)]
    wide = jnp.concatenate(
        [cinv[...].astype(BF16), jnp.zeros((cr, strip_w - cc), BF16)], axis=1
    )
    strip[pl.ds(pl.multiple_of(b * cr, 8), cr), :] = wide

    pl.semaphore_wait(barrier, n_plane - 1 + n_gx - 2 + len(DIAGONALS))

    start_copies = []
    for mine, (device, theirs) in ((1, (east, 0)), (3, (north, 2))):
        copy = remote(
            rows.at[face_rows(mine)],
            rows.at[face_rows(theirs)],
            face_send.at[mine],
            face_recv.at[theirs],
            device,
        )
        copy.start()
        start_copies.append(copy)

    plane_send(name_msg, name_plane, name_send.at[0], name_recv.at[0])

    @pl.loop(1, n_gx)
    def _(k):
        other = lax.rem(a + k, n_gx)
        remote(
            name_msg,
            name_gx.at[c * n_z + z],
            name_send.at[1],
            name_recv.at[1],
            {"gx": other, "gy": b},
        ).start()

    @pl.loop(1, n_gy)
    def _(k):
        other = lax.rem(b + k, n_gy)
        remote(my_strip, my_strip, strip_send, strip_recv, {"gx": a, "gy": other}).start()

    bt_copies = exchange(bt_send, bt_recv, face_send.at[pl.ds(4, 4)], face_recv.at[pl.ds(4, 4)])

    def coarse_start(k, local_rows, sums):
        primal = jnp.dot(basis16, local_rows, preferred_element_type=F32)
        for j, value in enumerate(sums):
            at = lax.broadcasted_iota(jnp.int32, primal.shape, 0) == n_primal + j
            primal = jnp.where(at, value, primal)
        message = primal.astype(BF16)
        g_msg[k] = message
        g_buf[k, slot] = message
        plane_send(g_msg.at[k], g_buf.at[k], stage_send.at[k, 0], stage_recv.at[k, 0])
        t_val[k] = jnp.dot(linv[...], local_rows, preferred_element_type=F32)
        return exchange(t_val.at[k], t_recv.at[k], t_ssem.at[k], t_rsem.at[k])

    def operate(k):
        finish(t_copies[k])
        joined = (t_val[k] + t_recv[k]) * masks[...]
        t_hat[k] = joined
        high = joined.astype(BF16)
        rest = (joined - high.astype(F32)).astype(BF16)
        s_val[k] = jnp.dot(schur[...], high, preferred_element_type=F32) + jnp.dot(
            schur[...], rest, preferred_element_type=F32
        )
        return exchange(s_val.at[k], s_recv.at[k], s_ssem.at[k], s_rsem.at[k])

    def operated(k):
        finish(s_copies[k])
        s_hat[k] = (s_val[k] + s_recv[k]) * masks[...]

    def coarse_scatter(k):
        wait_bytes(g_buf.at[k], n_plane - 1, stage_recv.at[k, 0])
        gathered = g_buf[k].reshape(n_plane * TILE, load_cases)
        part = jnp.dot(sel_t[...], gathered, preferred_element_type=F32)
        part = part.reshape(n_z, 8, load_cases)
        xs[k] = part
        xr[k, z] = xs[k, z]
        z_send(xs.at[k], xr.at[k], stage_send.at[k, 1], stage_recv.at[k, 1])

    def coarse_gather(k):
        wait_bytes(xr.at[k], n_z - 1, stage_recv.at[k, 1])
        mine = jnp.sum(xr[k], axis=0)
        x_msg[k] = mine
        xb[k, slot] = mine
        plane_send(x_msg.at[k], xb.at[k], stage_send.at[k, 2], stage_recv.at[k, 2])

    def coarse_solve(k):
        wait_bytes(xb.at[k], n_plane - 1, stage_recv.at[k, 2])
        low = xb[k, 0:n_gy].reshape(strip_w, load_cases).astype(BF16)
        high = xb[k, n_gy:].reshape(strip_w, load_cases).astype(BF16)
        part = jnp.dot(c2[0], low, preferred_element_type=F32) + jnp.dot(
            c2[1], high, preferred_element_type=F32
        )
        ys[k] = part.astype(BF16).reshape(n_z, TILE, load_cases)
        yr[k, z] = ys[k, z]
        z_send(ys.at[k], yr.at[k], stage_send.at[k, 3], stage_recv.at[k, 3])

    def coarse_direct(k):
        wait_bytes(g_buf.at[k], n_plane - 1, stage_recv.at[k, 0])
        gathered = g_buf[k].reshape(n_plane * TILE, load_cases)
        part = jnp.dot(c_full[...], gathered, preferred_element_type=F32)
        at = lax.rem(lax.broadcasted_iota(jnp.int32, part.shape, 0), TILE)
        rest = part - part.astype(BF16).astype(F32)
        part = jnp.where((at == n_primal + 1) | (at == n_primal + 3), rest, part)
        ys[k] = part.astype(BF16).reshape(n_z, TILE, load_cases)
        yr[k, z] = ys[k, z]
        z_send(ys.at[k], yr.at[k], stage_send.at[k, 3], stage_recv.at[k, 3])

    def coarse_finish(k):
        wait_bytes(yr.at[k], n_z - 1, stage_recv.at[k, 3])
        total = jnp.sum(yr[k].astype(F32), axis=0)
        pk[k, 0:TILE] = total.astype(BF16)
        offsets = OFFSETS if k + 1 < SOLVES else OFFSETS[:4:2]
        for at, offset in enumerate(OFFSETS):
            if offset in offsets:
                back = OFFSETS.index((-offset[0], -offset[1]))
                remote(
                    pk.at[k, pl.ds(0, TILE)],
                    pk.at[k, pl.ds((1 + back) * TILE, TILE)],
                    p_ssem.at[k],
                    p_rsem.at[k],
                    grid_peer(offset),
                ).start()
        first = total[n_primal : n_primal + 1] + total[n_primal + 1 : n_primal + 2]
        second = total[n_primal + 2 : n_primal + 3] + total[n_primal + 3 : n_primal + 4]
        return len(offsets), first, second

    def wait_tiles(k, count, sem):
        part = pk.at[k, pl.ds(TILE, count * TILE)]
        pltpu.make_async_copy(part, part, sem.at[k]).wait()

    def owned(first, second):
        total = first * second
        east_part = jnp.sum(total[face : 2 * face], axis=0, keepdims=True)
        north_part = jnp.sum(total[3 * face :], axis=0, keepdims=True)
        return east_part + north_part

    def split(value):
        high = value.astype(BF16).astype(F32)
        return high, value - high

    finish(start_copies)
    load_linv.wait()
    t_copies = []
    s_copies = []
    t_copies.append(coarse_start(0, rows[...], []))

    wait_bytes(name_plane, n_plane - 1, name_recv.at[0])
    plane_names = name_plane[...].reshape(n_plane * TILE, name_msg.shape[1]).astype(F32)
    plane_names = plane_names[:, 0:1] * 64.0 + plane_names[:, half : half + 1]
    target = lax.broadcasted_iota(jnp.int32, (1, 8 * n_z), 1)
    place = 8 * b + lax.rem(target, 8)
    wanted = jnp.where(place < cc, cc * (2 * (target // 8) + c) + place, CODE + place - cc)
    hits = jnp.where(plane_names == wanted.astype(F32), 1.0, 0.0).astype(F32)
    sel_t[...] = hits.T.astype(BF16)

    coarse_scatter(0)

    wait_bytes(name_gx, n_gx - 1, name_recv.at[1])
    gx_names = name_gx[...].reshape(n_gx * TILE, name_msg.shape[1]).astype(F32)
    gx_names = gx_names[:, 0:1] * 64.0 + gx_names[:, half : half + 1]

    width = c_nat.shape[2]
    face_cols = 3 * n_gy
    lanes = lax.broadcasted_iota(jnp.int32, (TILE, width), 1)
    prim = lax.broadcasted_iota(jnp.int32, (TILE, width), 0)
    within = 3 * b + lax.rem(prim, 3)
    low_face = jnp.where(prim < 3, 0, jnp.where(prim < 6, 1, 3))
    high_face = jnp.where(prim < 6, 2, 4)
    owned_prim = ((prim >= 3) & (prim < 6)) | ((prim >= 9) & (prim < 12))
    low_hit = (lanes == low_face * face_cols + within) & (owned_prim | (prim < 3))
    high_hit = (lanes == high_face * face_cols + within) & owned_prim
    spread_names = jnp.broadcast_to(gx_names, (n_gx * TILE, width)).reshape(
        n_gx, TILE, width
    )
    lane_names = jnp.sum(
        jnp.where(low_hit[None], spread_names[:n_z], 0.0)
        + jnp.where(high_hit[None], spread_names[n_z:], 0.0),
        axis=1,
    )
    name_lane_msg[...] = lane_names
    name_cols[b] = lane_names

    @pl.loop(1, n_gy)
    def _(k):
        remote(
            name_lane_msg,
            name_cols.at[b],
            perm_send.at[0],
            perm_recv.at[0],
            {"gx": a, "gy": lax.rem(b + k, n_gy)},
        ).start()

    wait_bytes(strip.reshape(n_gy, cr, strip_w), n_gy - 1, strip_recv)
    chunk = 256 if nc % 256 == 0 else nc // 3
    column = lax.broadcasted_iota(jnp.int32, (1, chunk), 1).astype(F32)

    def select(step, total):
        base = pl.multiple_of(step * chunk, chunk)
        hit = jnp.where(gx_names - (base * 1.0) == column, 1.0, 0.0).astype(BF16)
        return total + jnp.dot(hit, strip[pl.ds(base, chunk), :], preferred_element_type=F32)

    chosen = lax.fori_loop(
        0, nc // chunk, select, jnp.zeros((n_gx * TILE, strip_w), F32)
    )
    tsel[...] = chosen.astype(BF16).reshape(2, n_z * TILE, strip_w)
    c2[c] = tsel[c]
    c2_copy = remote(
        tsel.at[1 - c], c2.at[c], c2_send, c2_recv, {"gx": 2 * z + 1 - c, "gy": b}
    )
    c2_copy.start()
    c_own[a] = tsel[c, pl.ds(pl.multiple_of(z * TILE, TILE), TILE)]

    def send_rows(core, other):
        remote(
            tsel.at[core, pl.ds(pl.multiple_of(other * TILE, TILE), TILE)],
            c_own.at[a],
            perm_send.at[1],
            perm_recv.at[1],
            {"gx": 2 * other + core, "gy": b},
        ).start()

    @pl.loop(0, n_z - 1)
    def _(step):
        other = line_peer(step)
        send_rows(0, other)
        send_rows(1, other)

    send_rows(1 - c, z)

    finish(bt_copies)
    bb[...] = bb[...] + bt_recv[...]
    masks[0:face, :] = jnp.broadcast_to(
        bt_recv[0:face, MASK_LANE : MASK_LANE + 1].astype(F32), (face, load_cases)
    )
    masks[2 * face : 3 * face, :] = jnp.broadcast_to(
        bt_recv[2 * face : 3 * face, MASK_LANE : MASK_LANE + 1].astype(F32),
        (face, load_cases),
    )
    load_schur.wait()
    s_copies.append(operate(0))
    coarse_gather(0)

    from_row = lax.broadcasted_iota(jnp.int32, (BT_LANES, SLOT_LANES), 0)
    to_lane = lax.broadcasted_iota(jnp.int32, (BT_LANES, SLOT_LANES), 1)
    for at in range(4):
        to_slot = jnp.where(from_row < TILE, 0, at + 1)
        hit = (to_lane == TILE * to_slot + lax.rem(from_row, TILE)) & (from_row < 2 * TILE)
        move = jnp.where(hit, 1.0, 0.0).astype(BF16)
        here = face_rows(at)
        moved = jnp.dot(bb[here, :], move, preferred_element_type=F32)
        g_mat[here, :] = jnp.where(masks[here, 0:1] > 0.5, moved, 0.0).astype(BF16)
    image = jnp.dot(schur[...], g_mat[:, 0:BT_LANES], preferred_element_type=F32)
    sg_send[...] = image.astype(BF16)
    sg_copies = exchange(sg_send, sg_recv, sg_ssem, sg_rsem)

    c2_copy.wait_recv()
    coarse_solve(0)

    wait_bytes(name_cols, n_gy - 1, perm_recv.at[0])
    col_names = jnp.sum(name_cols[...], axis=0)
    used = lax.broadcasted_iota(jnp.int32, col_names.shape, 1) < 5 * face_cols
    col_strip = ((col_names + 0.5) * (1.0 / cc)).astype(jnp.int32)
    col_low = col_names.astype(jnp.int32) - cc * col_strip
    tau_strip[...] = col_strip
    tau_low[...] = jnp.where(used, col_low, -1)
    wait_bytes(c_own, n_gx - 1, perm_recv.at[1])
    inner = lax.broadcasted_iota(jnp.int32, (strip_w, 1), 0)
    strips = lax.broadcasted_iota(jnp.int32, (n_gx, 1, 1), 0)

    @pl.loop(0, n_z)
    def _(step):
        picks = jnp.where(inner == tau_low[pl.ds(step, 1), :], 1.0, 0.0).astype(BF16)
        mine = c_own[...].reshape(n_gx * TILE, strip_w)
        wide_rows = jnp.dot(mine, picks, preferred_element_type=F32)
        wide_rows = wide_rows.reshape(n_gx, TILE, width)
        hit = strips == tau_strip[pl.ds(step, 1), :][None]
        c_nat[step] = jnp.sum(jnp.where(hit, wide_rows, 0.0), axis=0).astype(BF16)

    c_line[z] = c_nat[z]
    z_send(c_nat, c_line, perm_send.at[2], perm_recv.at[2])

    finish(sg_copies)
    for at in range(4):
        to_slot = jnp.full(from_row.shape, -1, jnp.int32)
        for mine, theirs in enumerate(SEEN[at]):
            to_slot = jnp.where(from_row // TILE == mine, theirs, to_slot)
        hit = to_lane == TILE * to_slot + lax.rem(from_row, TILE)
        move = jnp.where(hit & (to_slot >= 0), 1.0, 0.0).astype(BF16)
        here = face_rows(at)
        moved = jnp.dot(sg_recv[here, :], move, preferred_element_type=F32)
        stay = jnp.where(to_lane == from_row, 1.0, 0.0).astype(BF16)
        kept = jnp.dot(sg_send[here, :], stay, preferred_element_type=F32)
        h_mat[here, :] = jnp.where(masks[here, 0:1] > 0.5, moved + kept, 0.0).astype(BF16)
    operated(0)

    counts = [coarse_finish(0)[0]]
    wait_tiles(0, counts[0], p_rsem)
    first = t_hat[0] + jnp.dot(g_mat[...], pk[0], preferred_element_type=F32)
    image = s_hat[0] + jnp.dot(h_mat[...], pk[0], preferred_element_type=F32)
    v0[...] = first
    w0[...] = image
    start = rows[...].astype(F32)
    old, curve = owned(start, first), owned(first, image)

    t_copies.append(coarse_start(1, image.astype(BF16), [*split(old), *split(curve)]))

    wait_bytes(c_line, n_z - 1, perm_recv.at[2])
    at = lax.broadcasted_iota(jnp.int32, (1, n_plane * TILE), 1)
    at_slot, at_prim = at // TILE, lax.rem(at, TILE)
    at_core, at_b = at_slot // n_gy, lax.rem(at_slot, n_gy)
    at_face = jnp.where(
        at_prim < 3, at_core, jnp.where(at_prim < 6, 1 + at_core, 3 + at_core)
    )
    at_b = jnp.where((at_prim >= 6) & (at_prim < 9), lax.rem(at_b + n_gy - 1, n_gy), at_b)
    at_col = jnp.where(
        at_prim < 12, at_face * face_cols + 3 * at_b + lax.rem(at_prim, 3), -1
    )
    place = jnp.where(
        lax.broadcasted_iota(jnp.int32, (width, 1), 0) == at_col, 1.0, 0.0
    ).astype(BF16)
    block = jnp.dot(
        c_line[...].reshape(n_z * TILE, width), place, preferred_element_type=F32
    )
    row_prim = lax.rem(lax.broadcasted_iota(jnp.int32, (n_z * TILE, 1), 0), TILE)
    adds = (row_prim >= 12) & (at_prim >= 12) & (row_prim // 2 == at_prim // 2)
    c_full[...] = jnp.where(adds, 1.0, block).astype(BF16)

    coarse_direct(1)
    s_copies.append(operate(1))
    count, old, curve = coarse_finish(1)
    step = old / curve
    counts.append(count)
    operated(1)
    wait_tiles(1, count, p_rsem)
    part = t_hat[1] + jnp.dot(g_mat[...], pk[1], preferred_element_type=F32)
    v1[...] = part
    second = v0[...] - step * part
    z1[...] = second
    image = s_hat[1] + jnp.dot(h_mat[...], pk[1], preferred_element_type=F32)
    image = w0[...] - step * image
    residual = rows[...].astype(F32) - step * w0[...]
    new, second_curve = owned(residual, second), owned(second, image)

    t_copies.append(coarse_start(2, image.astype(BF16), [*split(new), *split(second_curve)]))
    coarse_direct(2)
    finish(t_copies[2])
    count, new, second_curve = coarse_finish(2)
    ratio = new / old
    step_two = new / (second_curve - ratio * ratio * curve)
    counts.append(count)
    wait_tiles(2, count, p_rsem)
    for half_at, at in enumerate((1, 3)):
        here = face_rows(at)
        there = pl.ds(half_at * face, face)
        part = (t_val[2, here, :] + t_recv[2, here, :]) * masks[here, :] + jnp.dot(
            g_mat[here, :], pk[2], preferred_element_type=F32
        )
        second = z1[here, :]
        direction = second + ratio * v0[here, :]
        sol_out[there, :] = step * v0[here, :] + step_two * direction
        pre_out[there, :] = second - step_two * (part + ratio * v1[here, :])

    for copy in start_copies + bt_copies + [c2_copy] + sg_copies:
        copy.wait_send()
    wait_bytes(name_plane, n_plane - 1, name_send.at[0])
    wait_bytes(name_gx, n_gx - 1, name_send.at[1])
    wait_bytes(strip.reshape(n_gy, cr, strip_w), n_gy - 1, strip_send)
    wait_bytes(name_cols, n_gy - 1, perm_send.at[0])
    wait_bytes(c_own, n_gx - 1, perm_send.at[1])
    wait_bytes(c_line, n_z - 1, perm_send.at[2])
    wait_bytes(xr.at[0], n_z - 1, stage_send.at[0, 1])
    wait_bytes(xb.at[0], n_plane - 1, stage_send.at[0, 2])
    for k in range(SOLVES):
        for copy in t_copies[k]:
            copy.wait_send()
        wait_tiles(k, counts[k], p_ssem)
        wait_bytes(g_buf.at[k], n_plane - 1, stage_send.at[k, 0])
        wait_bytes(yr.at[k], n_z - 1, stage_send.at[k, 3])
    for k in range(OPS):
        for copy in s_copies[k]:
            copy.wait_send()


def shards(
    n_gx, n_gy, loads, schur, local_inv, coarse_basis, coarse_index, face_nodes, coarse_inverse
):
    owned, cases = loads.shape[2:]
    local = schur.shape[-1]
    cr, cc = coarse_inverse.shape
    nc = cr * n_gy
    n_z = n_gx // 2
    n_plane = 2 * n_gy
    strip_w = 8 * n_gy
    dma = pltpu.SemaphoreType.DMA
    vmem = pl.BlockSpec(memory_space=pltpu.VMEM)
    smem = pl.BlockSpec(memory_space=pltpu.SMEM)
    anywhere = pl.BlockSpec(memory_space=pl.ANY)
    scratch = [
        pltpu.VMEM((local, local), BF16),
        pltpu.VMEM((local, local), BF16),
        pltpu.VMEM((BT_LANES, local), F32),
        pltpu.VMEM((local, BT_LANES), BF16),
        pltpu.VMEM((local, BT_LANES), BF16),
        pltpu.VMEM((local, BT_LANES), BF16),
        pltpu.VMEM((local, cases), F32),
        pltpu.VMEM((local, cases), BF16),
        pltpu.VMEM((TILE, 128), BF16),
        pltpu.VMEM((n_plane, TILE, 128), BF16),
        pltpu.VMEM((n_gx, TILE, 128), BF16),
        pltpu.VMEM((8 * n_z, n_plane * TILE), BF16),
        pltpu.VMEM((nc, strip_w), BF16),
        pltpu.VMEM((2, n_z * TILE, strip_w), BF16),
        pltpu.VMEM((2, n_z * TILE, strip_w), BF16),
        pltpu.VMEM((n_gx, TILE, strip_w), BF16),
        pltpu.VMEM((n_gy, n_z, 16 * n_gy), F32),
        pltpu.VMEM((n_z, 16 * n_gy), F32),
        pltpu.VMEM((n_z, 16 * n_gy), jnp.int32),
        pltpu.VMEM((n_z, 16 * n_gy), jnp.int32),
        pltpu.VMEM((n_z, TILE, 16 * n_gy), BF16),
        pltpu.VMEM((n_z, TILE, 16 * n_gy), BF16),
        pltpu.VMEM((n_z * TILE, n_plane * TILE), BF16),
        pltpu.VMEM((SOLVES, local, cases), F32),
        pltpu.VMEM((SOLVES, local, cases), F32),
        pltpu.VMEM((OPS, local, cases), F32),
        pltpu.VMEM((OPS, local, cases), F32),
        pltpu.VMEM((OPS, local, cases), F32),
        pltpu.VMEM((OPS, local, cases), F32),
        pltpu.VMEM((local, BT_LANES), BF16),
        pltpu.VMEM((local, BT_LANES), BF16),
        pltpu.VMEM((local, SLOT_LANES), BF16),
        pltpu.VMEM((local, SLOT_LANES), BF16),
        pltpu.VMEM((SOLVES, TILE, cases), BF16),
        pltpu.VMEM((SOLVES, n_plane, TILE, cases), BF16),
        pltpu.VMEM((SOLVES, n_z, 8, cases), F32),
        pltpu.VMEM((SOLVES, n_z, 8, cases), F32),
        pltpu.VMEM((SOLVES, 8, cases), F32),
        pltpu.VMEM((SOLVES, n_plane, 8, cases), F32),
        pltpu.VMEM((SOLVES, n_z, TILE, cases), BF16),
        pltpu.VMEM((SOLVES, n_z, TILE, cases), BF16),
        pltpu.VMEM((SOLVES, SLOT_LANES, cases), BF16),
        pltpu.VMEM((local, cases), F32),
        pltpu.VMEM((local, cases), F32),
        pltpu.VMEM((local, cases), F32),
        pltpu.VMEM((local, cases), F32),
        dma((2,)),
        dma((8,)),
        dma((8,)),
        dma((2,)),
        dma((2,)),
        dma,
        dma,
        dma,
        dma,
        dma((3,)),
        dma((3,)),
        dma((SOLVES, 4)),
        dma((SOLVES, 4)),
        dma((SOLVES, 4)),
        dma((SOLVES, 4)),
        dma((OPS, 4)),
        dma((OPS, 4)),
        dma((4,)),
        dma((4,)),
        dma((SOLVES,)),
        dma((SOLVES,)),
    ]
    solution, precond = pl.pallas_call(
        functools.partial(kernel, n_gx, n_gy),
        out_shape=(
            jax.ShapeDtypeStruct((owned, cases), F32),
            jax.ShapeDtypeStruct((owned, cases), F32),
        ),
        in_specs=[vmem, anywhere, anywhere, vmem, smem, smem, vmem],
        out_specs=(vmem, vmem),
        scratch_shapes=scratch,
        compiler_params=pltpu.CompilerParams(
            collective_id=0, has_side_effects=True, vmem_limit_bytes=60 * 1024 * 1024
        ),
        name="bddc_cg",
    )(
        loads[0, 0],
        schur[0, 0],
        local_inv[0, 0],
        coarse_basis[0, 0],
        coarse_index[0, 0],
        face_nodes[0, 0],
        coarse_inverse,
    )
    return solution[None, None], precond[None, None]


def solution(mesh):
    placed = (
        P("gx", "gy", None, None),
        P("gx", "gy", None, None),
        P("gx", "gy", None, None),
        P("gx", "gy", None, None),
        P("gx", "gy", None),
        P("gx", "gy", None),
        P("gy", "gx"),
    )
    return jax.shard_map(
        functools.partial(shards, mesh.shape["gx"], mesh.shape["gy"]),
        mesh=mesh,
        in_specs=placed,
        out_specs=(P("gx", "gy", None, None), P("gx", "gy", None, None)),
        check_vma=False,
    )
```

```python
import functools
import math
import jax
import jax.numpy as jnp
from jax import lax
from jax.experimental import pallas as pl
from jax.experimental.pallas import tpu as pltpu
from jax.sharding import PartitionSpec as P

MESH = pl.DeviceIdType.MESH
F32 = jnp.float32
BF16 = jnp.bfloat16
TILE = 16
CODE = 4096
MASK_LANE = 64
BT_LANES = 128
SOLVES = 3
OPS = 2
SLOT_LANES = 256
OFFSETS = (
    (-1, 0),
    (1, 0),
    (0, -1),
    (0, 1),
    (-2, 0),
    (2, 0),
    (0, -2),
    (0, 2),
    (-1, -1),
    (-1, 1),
    (1, -1),
    (1, 1),
)
DIAGONALS = OFFSETS[8:]
SEEN = ((1, 5, 0, 9, 10), (2, 0, 6, 11, 12), (3, 9, 11, 7, 0), (4, 10, 12, 0, 8))


def kernel(
    n_gx,
    n_gy,
    loads,
    schur_hbm,
    linv_hbm,
    basis,
    index,
    nodes,
    cinv,
    sol_out,
    pre_out,
    schur,
    linv,
    bpad,
    bt_send,
    bt_recv,
    bb,
    masks,
    rows,
    name_msg,
    name_plane,
    name_gx,
    sel_t,
    strip_x,
    strip_y,
    tsel,
    c2,
    c_own,
    name_cols,
    name_lane_msg,
    tau_strip,
    tau_low,
    c_nat,
    c_line,
    c_full,
    t_val,
    t_recv,
    t_hat,
    s_val,
    s_recv,
    s_hat,
    sg_send,
    sg_recv,
    g_mat,
    h_mat,
    g_msg,
    g_buf,
    xs,
    xr,
    x_msg,
    xb,
    ys,
    yr,
    pk,
    v0,
    v1,
    z1,
    w0,
    load_sem,
    face_send,
    face_recv,
    name_send,
    name_recv,
    strip_send,
    strip_recv,
    c2_send,
    c2_recv,
    perm_send,
    perm_recv,
    stage_send,
    stage_recv,
    t_ssem,
    t_rsem,
    s_ssem,
    s_rsem,
    sg_ssem,
    sg_rsem,
    p_ssem,
    p_rsem,
):
    a = lax.axis_index("gx")
    b = lax.axis_index("gy")
    n_z = n_gx // 2
    n_plane = 2 * n_gy
    z = a // 2
    c = lax.rem(a, 2)
    slot = c * n_gy + b
    local = schur.shape[0]
    face = local // 4
    nodes_per = face // 3
    cr, cc = cinv.shape
    strip_w = 8 * n_gy
    load_cases = loads.shape[1]

    side = math.isqrt(n_gy)

    def far_first(step, extent):
        half = (step + 1) // 2
        return extent // 2 + jnp.where(lax.rem(step, 2) == 1, -half, half)

    def plane_peer(step, other_core):
        y = lax.rem(b // side + far_first(step // side, side), side)
        x = lax.rem(lax.rem(b, side) + far_first(lax.rem(step, side), side), side)
        return {"gx": 2 * z + lax.rem(c + other_core, 2), "gy": y * side + x}

    def line_peer(step):
        return lax.rem(z + far_first(step, n_z), n_z)

    def signal(device):
        pl.semaphore_signal(barrier, inc=1, device_id=device, device_id_type=MESH)

    barrier = pltpu.get_barrier_semaphore()
    pk[...] = jnp.zeros_like(pk)

    @pl.loop(0, n_z - 1)
    def _(step):
        other = line_peer(step)
        signal({"gx": 2 * other, "gy": b})
        signal({"gx": 2 * other + 1, "gy": b})

    @pl.loop(0, n_gy - 1)
    def _(step):
        signal(plane_peer(step, 0))
        signal(plane_peer(step, 1))

    signal(plane_peer(n_gy - 1, 1))

    def grid_peer(offset):
        return {
            "gx": lax.rem(a + offset[0] + n_gx, n_gx),
            "gy": lax.rem(b + offset[1] + n_gy, n_gy),
        }

    for offset in DIAGONALS:
        signal(grid_peer(offset))

    load_linv = pltpu.make_async_copy(linv_hbm, linv, load_sem.at[0])
    load_schur = pltpu.make_async_copy(schur_hbm, schur, load_sem.at[1])
    load_linv.start()
    load_schur.start()

    def remote(src, dst, send, recv, device):
        return pltpu.make_async_remote_copy(
            src_ref=src,
            dst_ref=dst,
            send_sem=send,
            recv_sem=recv,
            device_id=device,
            device_id_type=MESH,
        )

    def plane_send(src, dst, send, recv):
        @pl.loop(0, n_gy - 1)
        def _(step):
            remote(src, dst.at[slot], send, recv, plane_peer(step, 0)).start()
            remote(src, dst.at[slot], send, recv, plane_peer(step, 1)).start()

        remote(src, dst.at[slot], send, recv, plane_peer(n_gy - 1, 1)).start()

    def z_send(src, dst, send, recv):
        @pl.loop(0, n_z - 1)
        def _(step):
            other = line_peer(step)
            remote(
                src.at[other], dst.at[z], send, recv, {"gx": 2 * other + c, "gy": b}
            ).start()

    def wait_bytes(buf, count, sem):
        part = buf.at[pl.ds(0, count)]
        pltpu.make_async_copy(part, part, sem).wait()

    west = {"gx": lax.rem(a + n_gx - 1, n_gx), "gy": b}
    east = {"gx": lax.rem(a + 1, n_gx), "gy": b}
    south = {"gx": a, "gy": lax.rem(b + n_gy - 1, n_gy)}
    north = {"gx": a, "gy": lax.rem(b + 1, n_gy)}
    neighbours = ((west, 1), (east, 0), (south, 3), (north, 2))

    def face_rows(which):
        return pl.ds(which * face, face)

    def exchange(src, dst, send, recv):
        copies = []
        for mine, (device, theirs) in enumerate(neighbours):
            copies.append(
                remote(
                    src.at[face_rows(mine)],
                    dst.at[face_rows(theirs)],
                    send.at[mine],
                    recv.at[theirs],
                    device,
                )
            )
        for copy in copies:
            copy.start()
        return copies

    def finish(copies):
        for copy in copies:
            copy.wait_recv()

    lane = lax.broadcasted_iota(jnp.int32, (1, local), 1)
    which = lane // face
    node = lax.rem(lax.rem(lane, face), nodes_per)
    alive_east = (which == 1) & (node < nodes[0]) & (a < n_gx - 1)
    alive_north = (which == 3) & (node < nodes[1]) & (b < n_gy - 1)
    mask_row = jnp.where(alive_east | alive_north, 1.0, 0.0).astype(F32)
    basis_wide = basis[...].astype(F32)
    n_primal = basis_wide.shape[0]

    bpad[...] = jnp.zeros_like(bpad)
    bpad[TILE : TILE + n_primal, :] = basis_wide
    bpad[MASK_LANE : MASK_LANE + 1, :] = mask_row
    flipped = bpad[...].T
    bt_send[...] = flipped.astype(BF16)
    masks[...] = jnp.broadcast_to(flipped[:, MASK_LANE : MASK_LANE + 1], masks.shape)
    bpad[...] = jnp.zeros_like(bpad)
    bpad[0:n_primal, :] = basis_wide
    bb[...] = bpad[...].T.astype(BF16)
    basis16 = bpad[0:TILE, :].astype(BF16)

    rows[face : 2 * face, :] = (
        loads[0:face, :].astype(F32) * masks[face : 2 * face, :]
    ).astype(BF16)
    rows[3 * face :, :] = (
        loads[face:, :].astype(F32) * masks[3 * face :, :]
    ).astype(BF16)

    name_row = lax.broadcasted_iota(jnp.int32, name_msg.shape, 0)
    name_lane = lax.broadcasted_iota(jnp.int32, name_msg.shape, 1)
    names = CODE + name_row - n_primal
    for j in range(n_primal):
        names = jnp.where(name_row == j, index[j], names)
    half = name_msg.shape[1] // 2
    name_msg[...] = (
        jnp.where(name_lane < half, names // 64, lax.rem(names, 64)).astype(F32).astype(BF16)
    )
    name_plane[slot] = name_msg[...]
    name_gx[c * n_z + z] = name_msg[...]

    half_cr = cr // 2
    row_y, row_x = b // side, lax.rem(b, side)
    wide = jnp.concatenate(
        [cinv[...].astype(BF16), jnp.zeros((cr, strip_w - cc), BF16)], axis=1
    )
    strip_x[b] = wide[:half_cr]
    strip_y[row_x * side + row_y] = wide[half_cr:]

    pl.semaphore_wait(barrier, n_plane - 1 + n_gx - 2 + len(DIAGONALS))

    start_copies = []
    for mine, (device, theirs) in ((1, (east, 0)), (3, (north, 2))):
        copy = remote(
            rows.at[face_rows(mine)],
            rows.at[face_rows(theirs)],
            face_send.at[mine],
            face_recv.at[theirs],
            device,
        )
        copy.start()
        start_copies.append(copy)

    plane_send(name_msg, name_plane, name_send.at[0], name_recv.at[0])

    @pl.loop(1, n_gx)
    def _(k):
        other = lax.rem(a + k, n_gx)
        remote(
            name_msg,
            name_gx.at[c * n_z + z],
            name_send.at[1],
            name_recv.at[1],
            {"gx": other, "gy": b},
        ).start()

    def along_x(step):
        x = lax.rem(row_x + far_first(step, side), side)
        return {"gx": a, "gy": row_y * side + x}

    def along_y(step):
        y = lax.rem(row_y + far_first(step, side), side)
        return {"gx": a, "gy": y * side + row_x}

    def strip_pass(which, first_x, count_x, first_y, count_y):
        here_x = strip_x.at[pl.ds(first_x, count_x)]
        here_y = strip_y.at[pl.ds(first_y, count_y)]
        ways = (along_x, along_y) if which == 0 else (along_y, along_x)

        @pl.loop(0, side - 1)
        def _(step):
            at = 2 * which
            remote(here_x, here_x, strip_send.at[at], strip_recv.at[at], ways[0](step)).start()
            remote(
                here_y, here_y, strip_send.at[at + 1], strip_recv.at[at + 1], ways[1](step)
            ).start()

    def strip_wait(which, sem):
        count = (side - 1) * (side if which else 1)
        wait_bytes(strip_x, count, sem.at[2 * which])
        wait_bytes(strip_y, count, sem.at[2 * which + 1])

    strip_pass(0, b, 1, row_x * side + row_y, 1)

    def coarse_start(k, local_rows, sums):
        primal = jnp.dot(basis16, local_rows, preferred_element_type=F32)
        for j, value in enumerate(sums):
            at = lax.broadcasted_iota(jnp.int32, primal.shape, 0) == n_primal + j
            primal = jnp.where(at, value, primal)
        message = primal.astype(BF16)
        g_msg[k] = message
        g_buf[k, slot] = message
        plane_send(g_msg.at[k], g_buf.at[k], stage_send.at[k, 0], stage_recv.at[k, 0])
        if k == 0:
            strip_wait(0, strip_recv)
            strip_pass(1, row_y * side, side, row_x * side, side)
        t_val[k] = jnp.dot(linv[...], local_rows, preferred_element_type=F32)

    def local_start(k):
        return exchange(t_val.at[k], t_recv.at[k], t_ssem.at[k], t_rsem.at[k])

    def operate(k):
        finish(t_copies[k])
        joined = (t_val[k] + t_recv[k]) * masks[...]
        t_hat[k] = joined
        high = joined.astype(BF16)
        rest = (joined - high.astype(F32)).astype(BF16)
        s_val[k] = jnp.dot(schur[...], high, preferred_element_type=F32) + jnp.dot(
            schur[...], rest, preferred_element_type=F32
        )
        return exchange(s_val.at[k], s_recv.at[k], s_ssem.at[k], s_rsem.at[k])

    def operated(k):
        finish(s_copies[k])
        s_hat[k] = (s_val[k] + s_recv[k]) * masks[...]

    def coarse_scatter(k):
        wait_bytes(g_buf.at[k], n_plane - 1, stage_recv.at[k, 0])
        gathered = g_buf[k].reshape(n_plane * TILE, load_cases)
        part = jnp.dot(sel_t[...], gathered, preferred_element_type=F32)
        part = part.reshape(n_z, 8, load_cases)
        xs[k] = part
        xr[k, z] = xs[k, z]
        z_send(xs.at[k], xr.at[k], stage_send.at[k, 1], stage_recv.at[k, 1])

    def coarse_gather(k):
        wait_bytes(xr.at[k], n_z - 1, stage_recv.at[k, 1])
        mine = jnp.sum(xr[k], axis=0)
        x_msg[k] = mine
        xb[k, slot] = mine
        plane_send(x_msg.at[k], xb.at[k], stage_send.at[k, 2], stage_recv.at[k, 2])

    def coarse_solve(k):
        wait_bytes(xb.at[k], n_plane - 1, stage_recv.at[k, 2])
        low = xb[k, 0:n_gy].reshape(strip_w, load_cases).astype(BF16)
        high = xb[k, n_gy:].reshape(strip_w, load_cases).astype(BF16)
        part = jnp.dot(c2[0], low, preferred_element_type=F32) + jnp.dot(
            c2[1], high, preferred_element_type=F32
        )
        ys[k] = part.astype(BF16).reshape(n_z, TILE, load_cases)
        yr[k, z] = ys[k, z]
        z_send(ys.at[k], yr.at[k], stage_send.at[k, 3], stage_recv.at[k, 3])

    def coarse_direct(k):
        wait_bytes(g_buf.at[k], n_plane - 1, stage_recv.at[k, 0])
        gathered = g_buf[k].reshape(n_plane * TILE, load_cases)
        part = jnp.dot(c_full[...], gathered, preferred_element_type=F32)
        at = lax.rem(lax.broadcasted_iota(jnp.int32, part.shape, 0), TILE)
        rest = part - part.astype(BF16).astype(F32)
        part = jnp.where((at == n_primal + 1) | (at == n_primal + 3), rest, part)
        ys[k] = part.astype(BF16).reshape(n_z, TILE, load_cases)
        yr[k, z] = ys[k, z]
        z_send(ys.at[k], yr.at[k], stage_send.at[k, 3], stage_recv.at[k, 3])

    def coarse_finish(k):
        wait_bytes(yr.at[k], n_z - 1, stage_recv.at[k, 3])
        total = jnp.sum(yr[k].astype(F32), axis=0)
        pk[k, 0:TILE] = total.astype(BF16)
        offsets = OFFSETS if k + 1 < SOLVES else OFFSETS[:4:2]
        for at, offset in enumerate(OFFSETS):
            if offset in offsets:
                back = OFFSETS.index((-offset[0], -offset[1]))
                remote(
                    pk.at[k, pl.ds(0, TILE)],
                    pk.at[k, pl.ds((1 + back) * TILE, TILE)],
                    p_ssem.at[k],
                    p_rsem.at[k],
                    grid_peer(offset),
                ).start()
        first = total[n_primal : n_primal + 1] + total[n_primal + 1 : n_primal + 2]
        second = total[n_primal + 2 : n_primal + 3] + total[n_primal + 3 : n_primal + 4]
        return len(offsets), first, second

    def wait_tiles(k, count, sem):
        part = pk.at[k, pl.ds(TILE, count * TILE)]
        pltpu.make_async_copy(part, part, sem.at[k]).wait()

    def owned(first, second):
        total = first * second
        east_part = jnp.sum(total[face : 2 * face], axis=0, keepdims=True)
        north_part = jnp.sum(total[3 * face :], axis=0, keepdims=True)
        return east_part + north_part

    def split(value):
        high = value.astype(BF16).astype(F32)
        return high, value - high

    finish(start_copies)
    load_linv.wait()
    t_copies = []
    s_copies = []
    coarse_start(0, rows[...], [])

    wait_bytes(name_plane, n_plane - 1, name_recv.at[0])
    plane_names = name_plane[...].reshape(n_plane * TILE, name_msg.shape[1]).astype(F32)
    plane_names = plane_names[:, 0:1] * 64.0 + plane_names[:, half : half + 1]
    target = lax.broadcasted_iota(jnp.int32, (1, 8 * n_z), 1)
    place = 8 * b + lax.rem(target, 8)
    wanted = jnp.where(place < cc, cc * (2 * (target // 8) + c) + place, CODE + place - cc)
    hits = jnp.where(plane_names == wanted.astype(F32), 1.0, 0.0).astype(F32)
    sel_t[...] = hits.T.astype(BF16)

    coarse_scatter(0)
    bt_copies = exchange(bt_send, bt_recv, face_send.at[pl.ds(4, 4)], face_recv.at[pl.ds(4, 4)])

    t_copies.append(local_start(0))

    wait_bytes(name_gx, n_gx - 1, name_recv.at[1])
    gx_names = name_gx[...].reshape(n_gx * TILE, name_msg.shape[1]).astype(F32)
    gx_names = gx_names[:, 0:1] * 64.0 + gx_names[:, half : half + 1]

    width = c_nat.shape[2]
    face_cols = 3 * n_gy
    lanes = lax.broadcasted_iota(jnp.int32, (TILE, width), 1)
    prim = lax.broadcasted_iota(jnp.int32, (TILE, width), 0)
    within = 3 * b + lax.rem(prim, 3)
    low_face = jnp.where(prim < 3, 0, jnp.where(prim < 6, 1, 3))
    high_face = jnp.where(prim < 6, 2, 4)
    owned_prim = ((prim >= 3) & (prim < 6)) | ((prim >= 9) & (prim < 12))
    low_hit = (lanes == low_face * face_cols + within) & (owned_prim | (prim < 3))
    high_hit = (lanes == high_face * face_cols + within) & owned_prim
    spread_names = jnp.broadcast_to(gx_names, (n_gx * TILE, width)).reshape(
        n_gx, TILE, width
    )
    lane_names = jnp.sum(
        jnp.where(low_hit[None], spread_names[:n_z], 0.0)
        + jnp.where(high_hit[None], spread_names[n_z:], 0.0),
        axis=1,
    )
    name_lane_msg[...] = lane_names
    name_cols[b] = lane_names

    @pl.loop(1, n_gy)
    def _(k):
        remote(
            name_lane_msg,
            name_cols.at[b],
            perm_send.at[0],
            perm_recv.at[0],
            {"gx": a, "gy": lax.rem(b + k, n_gy)},
        ).start()

    strip_wait(1, strip_recv)
    column = lax.broadcasted_iota(jnp.int32, (1, cr), 1)
    second_half = column >= half_cr

    def select(step, total):
        at = 2 * step
        at_x = jnp.where(second_half, cr * (at + 1) + column - half_cr, cr * at + column)
        low = lax.rem(at, side) * side + at // side
        at_y = jnp.where(
            second_half, cr * (low + side) + column, cr * low + column + half_cr
        )
        hit_x = jnp.where(gx_names == at_x.astype(F32), 1.0, 0.0).astype(BF16)
        hit_y = jnp.where(gx_names == at_y.astype(F32), 1.0, 0.0).astype(BF16)
        rows_x = strip_x[pl.ds(at, 2)].reshape(cr, strip_w)
        rows_y = strip_y[pl.ds(at, 2)].reshape(cr, strip_w)
        total = total + jnp.dot(hit_x, rows_x, preferred_element_type=F32)
        return total + jnp.dot(hit_y, rows_y, preferred_element_type=F32)

    chosen = lax.fori_loop(
        0, n_gy // 2, select, jnp.zeros((n_gx * TILE, strip_w), F32)
    )
    tsel[...] = chosen.astype(BF16).reshape(2, n_z * TILE, strip_w)
    c2[c] = tsel[c]
    c2_copy = remote(
        tsel.at[1 - c], c2.at[c], c2_send, c2_recv, {"gx": 2 * z + 1 - c, "gy": b}
    )
    c2_copy.start()
    c_own[a] = tsel[c, pl.ds(pl.multiple_of(z * TILE, TILE), TILE)]

    def send_rows(core, other):
        remote(
            tsel.at[core, pl.ds(pl.multiple_of(other * TILE, TILE), TILE)],
            c_own.at[a],
            perm_send.at[1],
            perm_recv.at[1],
            {"gx": 2 * other + core, "gy": b},
        ).start()

    @pl.loop(0, n_z - 1)
    def _(step):
        other = line_peer(step)
        send_rows(0, other)
        send_rows(1, other)

    send_rows(1 - c, z)

    coarse_gather(0)
    finish(bt_copies)
    bb[...] = bb[...] + bt_recv[...]
    masks[0:face, :] = jnp.broadcast_to(
        bt_recv[0:face, MASK_LANE : MASK_LANE + 1].astype(F32), (face, load_cases)
    )
    masks[2 * face : 3 * face, :] = jnp.broadcast_to(
        bt_recv[2 * face : 3 * face, MASK_LANE : MASK_LANE + 1].astype(F32),
        (face, load_cases),
    )
    load_schur.wait()
    s_copies.append(operate(0))

    from_row = lax.broadcasted_iota(jnp.int32, (BT_LANES, SLOT_LANES), 0)
    to_lane = lax.broadcasted_iota(jnp.int32, (BT_LANES, SLOT_LANES), 1)
    for at in range(4):
        to_slot = jnp.where(from_row < TILE, 0, at + 1)
        hit = (to_lane == TILE * to_slot + lax.rem(from_row, TILE)) & (from_row < 2 * TILE)
        move = jnp.where(hit, 1.0, 0.0).astype(BF16)
        here = face_rows(at)
        moved = jnp.dot(bb[here, :], move, preferred_element_type=F32)
        g_mat[here, :] = jnp.where(masks[here, 0:1] > 0.5, moved, 0.0).astype(BF16)
    image = jnp.dot(schur[...], g_mat[:, 0:BT_LANES], preferred_element_type=F32)
    sg_send[...] = image.astype(BF16)
    sg_copies = exchange(sg_send, sg_recv, sg_ssem, sg_rsem)

    c2_copy.wait_recv()
    coarse_solve(0)

    wait_bytes(name_cols, n_gy - 1, perm_recv.at[0])
    col_names = jnp.sum(name_cols[...], axis=0)
    used = lax.broadcasted_iota(jnp.int32, col_names.shape, 1) < 5 * face_cols
    col_strip = ((col_names + 0.5) * (1.0 / cc)).astype(jnp.int32)
    col_low = col_names.astype(jnp.int32) - cc * col_strip
    tau_strip[...] = col_strip
    tau_low[...] = jnp.where(used, col_low, -1)
    wait_bytes(c_own, n_gx - 1, perm_recv.at[1])
    inner = lax.broadcasted_iota(jnp.int32, (strip_w, 1), 0)
    strips = lax.broadcasted_iota(jnp.int32, (n_gx, 1, 1), 0)

    @pl.loop(0, n_z)
    def _(step):
        picks = jnp.where(inner == tau_low[pl.ds(step, 1), :], 1.0, 0.0).astype(BF16)
        mine = c_own[...].reshape(n_gx * TILE, strip_w)
        wide_rows = jnp.dot(mine, picks, preferred_element_type=F32)
        wide_rows = wide_rows.reshape(n_gx, TILE, width)
        hit = strips == tau_strip[pl.ds(step, 1), :][None]
        c_nat[step] = jnp.sum(jnp.where(hit, wide_rows, 0.0), axis=0).astype(BF16)

    c_line[z] = c_nat[z]
    z_send(c_nat, c_line, perm_send.at[2], perm_recv.at[2])

    finish(sg_copies)
    for at in range(4):
        to_slot = jnp.full(from_row.shape, -1, jnp.int32)
        for mine, theirs in enumerate(SEEN[at]):
            to_slot = jnp.where(from_row // TILE == mine, theirs, to_slot)
        hit = to_lane == TILE * to_slot + lax.rem(from_row, TILE)
        move = jnp.where(hit & (to_slot >= 0), 1.0, 0.0).astype(BF16)
        here = face_rows(at)
        moved = jnp.dot(sg_recv[here, :], move, preferred_element_type=F32)
        stay = jnp.where(to_lane == from_row, 1.0, 0.0).astype(BF16)
        kept = jnp.dot(sg_send[here, :], stay, preferred_element_type=F32)
        h_mat[here, :] = jnp.where(masks[here, 0:1] > 0.5, moved + kept, 0.0).astype(BF16)
    operated(0)

    counts = [coarse_finish(0)[0]]
    wait_tiles(0, counts[0], p_rsem)
    first = t_hat[0] + jnp.dot(g_mat[...], pk[0], preferred_element_type=F32)
    image = s_hat[0] + jnp.dot(h_mat[...], pk[0], preferred_element_type=F32)
    v0[...] = first
    w0[...] = image
    start = rows[...].astype(F32)
    old, curve = owned(start, first), owned(first, image)

    coarse_start(1, image.astype(BF16), [*split(old), *split(curve)])
    t_copies.append(local_start(1))

    wait_bytes(c_line, n_z - 1, perm_recv.at[2])
    at = lax.broadcasted_iota(jnp.int32, (1, n_plane * TILE), 1)
    at_slot, at_prim = at // TILE, lax.rem(at, TILE)
    at_core, at_b = at_slot // n_gy, lax.rem(at_slot, n_gy)
    at_face = jnp.where(
        at_prim < 3, at_core, jnp.where(at_prim < 6, 1 + at_core, 3 + at_core)
    )
    at_b = jnp.where((at_prim >= 6) & (at_prim < 9), lax.rem(at_b + n_gy - 1, n_gy), at_b)
    at_col = jnp.where(
        at_prim < 12, at_face * face_cols + 3 * at_b + lax.rem(at_prim, 3), -1
    )
    place = jnp.where(
        lax.broadcasted_iota(jnp.int32, (width, 1), 0) == at_col, 1.0, 0.0
    ).astype(BF16)
    block = jnp.dot(
        c_line[...].reshape(n_z * TILE, width), place, preferred_element_type=F32
    )
    row_prim = lax.rem(lax.broadcasted_iota(jnp.int32, (n_z * TILE, 1), 0), TILE)
    adds = (row_prim >= 12) & (at_prim >= 12) & (row_prim // 2 == at_prim // 2)
    c_full[...] = jnp.where(adds, 1.0, block).astype(BF16)

    coarse_direct(1)
    s_copies.append(operate(1))
    count, old, curve = coarse_finish(1)
    step = old / curve
    counts.append(count)
    operated(1)
    wait_tiles(1, count, p_rsem)
    part = t_hat[1] + jnp.dot(g_mat[...], pk[1], preferred_element_type=F32)
    v1[...] = part
    second = v0[...] - step * part
    z1[...] = second
    image = s_hat[1] + jnp.dot(h_mat[...], pk[1], preferred_element_type=F32)
    image = w0[...] - step * image
    residual = rows[...].astype(F32) - step * w0[...]
    new, second_curve = owned(residual, second), owned(second, image)

    coarse_start(2, image.astype(BF16), [*split(new), *split(second_curve)])
    t_copies.append(local_start(2))
    coarse_direct(2)
    finish(t_copies[2])
    count, new, second_curve = coarse_finish(2)
    ratio = new / old
    step_two = new / (second_curve - ratio * ratio * curve)
    counts.append(count)
    wait_tiles(2, count, p_rsem)
    for half_at, at in enumerate((1, 3)):
        here = face_rows(at)
        there = pl.ds(half_at * face, face)
        part = (t_val[2, here, :] + t_recv[2, here, :]) * masks[here, :] + jnp.dot(
            g_mat[here, :], pk[2], preferred_element_type=F32
        )
        second = z1[here, :]
        direction = second + ratio * v0[here, :]
        sol_out[there, :] = step * v0[here, :] + step_two * direction
        pre_out[there, :] = second - step_two * (part + ratio * v1[here, :])

    for copy in start_copies + bt_copies + [c2_copy] + sg_copies:
        copy.wait_send()
    wait_bytes(name_plane, n_plane - 1, name_send.at[0])
    wait_bytes(name_gx, n_gx - 1, name_send.at[1])
    strip_wait(0, strip_send)
    strip_wait(1, strip_send)
    wait_bytes(name_cols, n_gy - 1, perm_send.at[0])
    wait_bytes(c_own, n_gx - 1, perm_send.at[1])
    wait_bytes(c_line, n_z - 1, perm_send.at[2])
    wait_bytes(xr.at[0], n_z - 1, stage_send.at[0, 1])
    wait_bytes(xb.at[0], n_plane - 1, stage_send.at[0, 2])
    for k in range(SOLVES):
        for copy in t_copies[k]:
            copy.wait_send()
        wait_tiles(k, counts[k], p_ssem)
        wait_bytes(g_buf.at[k], n_plane - 1, stage_send.at[k, 0])
        wait_bytes(yr.at[k], n_z - 1, stage_send.at[k, 3])
    for k in range(OPS):
        for copy in s_copies[k]:
            copy.wait_send()


def shards(
    n_gx, n_gy, loads, schur, local_inv, coarse_basis, coarse_index, face_nodes, coarse_inverse
):
    owned, cases = loads.shape[2:]
    local = schur.shape[-1]
    cr, cc = coarse_inverse.shape
    n_z = n_gx // 2
    n_plane = 2 * n_gy
    strip_w = 8 * n_gy
    dma = pltpu.SemaphoreType.DMA
    vmem = pl.BlockSpec(memory_space=pltpu.VMEM)
    smem = pl.BlockSpec(memory_space=pltpu.SMEM)
    anywhere = pl.BlockSpec(memory_space=pl.ANY)
    scratch = [
        pltpu.VMEM((local, local), BF16),
        pltpu.VMEM((local, local), BF16),
        pltpu.VMEM((BT_LANES, local), F32),
        pltpu.VMEM((local, BT_LANES), BF16),
        pltpu.VMEM((local, BT_LANES), BF16),
        pltpu.VMEM((local, BT_LANES), BF16),
        pltpu.VMEM((local, cases), F32),
        pltpu.VMEM((local, cases), BF16),
        pltpu.VMEM((TILE, 128), BF16),
        pltpu.VMEM((n_plane, TILE, 128), BF16),
        pltpu.VMEM((n_gx, TILE, 128), BF16),
        pltpu.VMEM((8 * n_z, n_plane * TILE), BF16),
        pltpu.VMEM((n_gy, cr // 2, strip_w), BF16),
        pltpu.VMEM((n_gy, cr // 2, strip_w), BF16),
        pltpu.VMEM((2, n_z * TILE, strip_w), BF16),
        pltpu.VMEM((2, n_z * TILE, strip_w), BF16),
        pltpu.VMEM((n_gx, TILE, strip_w), BF16),
        pltpu.VMEM((n_gy, n_z, 16 * n_gy), F32),
        pltpu.VMEM((n_z, 16 * n_gy), F32),
        pltpu.VMEM((n_z, 16 * n_gy), jnp.int32),
        pltpu.VMEM((n_z, 16 * n_gy), jnp.int32),
        pltpu.VMEM((n_z, TILE, 16 * n_gy), BF16),
        pltpu.VMEM((n_z, TILE, 16 * n_gy), BF16),
        pltpu.VMEM((n_z * TILE, n_plane * TILE), BF16),
        pltpu.VMEM((SOLVES, local, cases), F32),
        pltpu.VMEM((SOLVES, local, cases), F32),
        pltpu.VMEM((OPS, local, cases), F32),
        pltpu.VMEM((OPS, local, cases), F32),
        pltpu.VMEM((OPS, local, cases), F32),
        pltpu.VMEM((OPS, local, cases), F32),
        pltpu.VMEM((local, BT_LANES), BF16),
        pltpu.VMEM((local, BT_LANES), BF16),
        pltpu.VMEM((local, SLOT_LANES), BF16),
        pltpu.VMEM((local, SLOT_LANES), BF16),
        pltpu.VMEM((SOLVES, TILE, cases), BF16),
        pltpu.VMEM((SOLVES, n_plane, TILE, cases), BF16),
        pltpu.VMEM((SOLVES, n_z, 8, cases), F32),
        pltpu.VMEM((SOLVES, n_z, 8, cases), F32),
        pltpu.VMEM((SOLVES, 8, cases), F32),
        pltpu.VMEM((SOLVES, n_plane, 8, cases), F32),
        pltpu.VMEM((SOLVES, n_z, TILE, cases), BF16),
        pltpu.VMEM((SOLVES, n_z, TILE, cases), BF16),
        pltpu.VMEM((SOLVES, SLOT_LANES, cases), BF16),
        pltpu.VMEM((local, cases), F32),
        pltpu.VMEM((local, cases), F32),
        pltpu.VMEM((local, cases), F32),
        pltpu.VMEM((local, cases), F32),
        dma((2,)),
        dma((8,)),
        dma((8,)),
        dma((2,)),
        dma((2,)),
        dma((4,)),
        dma((4,)),
        dma,
        dma,
        dma((3,)),
        dma((3,)),
        dma((SOLVES, 4)),
        dma((SOLVES, 4)),
        dma((SOLVES, 4)),
        dma((SOLVES, 4)),
        dma((OPS, 4)),
        dma((OPS, 4)),
        dma((4,)),
        dma((4,)),
        dma((SOLVES,)),
        dma((SOLVES,)),
    ]
    solution, precond = pl.pallas_call(
        functools.partial(kernel, n_gx, n_gy),
        out_shape=(
            jax.ShapeDtypeStruct((owned, cases), F32),
            jax.ShapeDtypeStruct((owned, cases), F32),
        ),
        in_specs=[vmem, anywhere, anywhere, vmem, smem, smem, vmem],
        out_specs=(vmem, vmem),
        scratch_shapes=scratch,
        compiler_params=pltpu.CompilerParams(
            collective_id=0, has_side_effects=True, vmem_limit_bytes=60 * 1024 * 1024
        ),
        name="bddc_cg",
    )(
        loads[0, 0],
        schur[0, 0],
        local_inv[0, 0],
        coarse_basis[0, 0],
        coarse_index[0, 0],
        face_nodes[0, 0],
        coarse_inverse,
    )
    return solution[None, None], precond[None, None]


def solution(mesh):
    placed = (
        P("gx", "gy", None, None),
        P("gx", "gy", None, None),
        P("gx", "gy", None, None),
        P("gx", "gy", None, None),
        P("gx", "gy", None),
        P("gx", "gy", None),
        P("gy", "gx"),
    )
    return jax.shard_map(
        functools.partial(shards, mesh.shape["gx"], mesh.shape["gy"]),
        mesh=mesh,
        in_specs=placed,
        out_specs=(P("gx", "gy", None, None), P("gx", "gy", None, None)),
        check_vma=False,
    )
```

```python
import functools
import math
import jax
import jax.numpy as jnp
from jax import lax
from jax.experimental import pallas as pl
from jax.experimental.pallas import tpu as pltpu
from jax.sharding import PartitionSpec as P

MESH = pl.DeviceIdType.MESH
F32 = jnp.float32
BF16 = jnp.bfloat16
TILE = 16
CODE = 4096
MASK_LANE = 64
BT_LANES = 128
SOLVES = 3
OPS = 2
SLOT_LANES = 256
OFFSETS = (
    (-1, 0),
    (1, 0),
    (0, -1),
    (0, 1),
    (-2, 0),
    (2, 0),
    (0, -2),
    (0, 2),
    (-1, -1),
    (-1, 1),
    (1, -1),
    (1, 1),
)
DIAGONALS = OFFSETS[8:]
SEEN = ((1, 5, 0, 9, 10), (2, 0, 6, 11, 12), (3, 9, 11, 7, 0), (4, 10, 12, 0, 8))


def kernel(
    n_gx,
    n_gy,
    loads,
    schur_hbm,
    linv_hbm,
    basis,
    index,
    nodes,
    cinv,
    sol_out,
    pre_out,
    schur,
    linv,
    bpad,
    bt_send,
    bt_recv,
    bb,
    masks,
    rows,
    name_msg,
    name_plane,
    name_gx,
    sel_t,
    strip_x,
    strip_y,
    tsel,
    c2,
    c_own,
    name_cols,
    name_lane_msg,
    tau_strip,
    tau_low,
    c_nat,
    c_line,
    c_full,
    t_val,
    t_recv,
    t_hat,
    s_val,
    s_recv,
    s_hat,
    sg_send,
    sg_recv,
    g_mat,
    h_mat,
    g_msg,
    g_buf,
    xs,
    xr,
    x_msg,
    xb,
    ys,
    yr,
    pk,
    v0,
    v1,
    z1,
    w0,
    load_sem,
    face_send,
    face_recv,
    name_send,
    name_recv,
    strip_send,
    strip_recv,
    c2_send,
    c2_recv,
    perm_send,
    perm_recv,
    stage_send,
    stage_recv,
    t_ssem,
    t_rsem,
    s_ssem,
    s_rsem,
    sg_ssem,
    sg_rsem,
    p_ssem,
    p_rsem,
):
    a = lax.axis_index("gx")
    b = lax.axis_index("gy")
    n_z = n_gx // 2
    n_plane = 2 * n_gy
    z = a // 2
    c = lax.rem(a, 2)
    slot = c * n_gy + b
    local = schur.shape[0]
    face = local // 4
    nodes_per = face // 3
    cr, cc = cinv.shape
    strip_w = 8 * n_gy
    load_cases = loads.shape[1]

    side = math.isqrt(n_gy)

    def far_first(step, extent):
        half = (step + 1) // 2
        if isinstance(step, int):
            return extent // 2 + (-half if step % 2 else half)
        return extent // 2 + jnp.where(lax.rem(step, 2) == 1, -half, half)

    def plane_peer(step, other_core):
        y = lax.rem(b // side + far_first(step // side, side), side)
        x = lax.rem(lax.rem(b, side) + far_first(step % side, side), side)
        return {"gx": 2 * z + lax.rem(c + other_core, 2), "gy": y * side + x}

    def line_peer(step):
        return lax.rem(z + far_first(step, n_z), n_z)

    def signal(device):
        pl.semaphore_signal(barrier, inc=1, device_id=device, device_id_type=MESH)

    barrier = pltpu.get_barrier_semaphore()
    pk[...] = jnp.zeros_like(pk)

    @pl.loop(0, n_z - 1)
    def _(step):
        other = line_peer(step)
        signal({"gx": 2 * other, "gy": b})
        signal({"gx": 2 * other + 1, "gy": b})

    @pl.loop(0, n_gy - 1)
    def _(step):
        signal(plane_peer(step, 0))
        signal(plane_peer(step, 1))

    signal(plane_peer(n_gy - 1, 1))

    def grid_peer(offset):
        return {
            "gx": lax.rem(a + offset[0] + n_gx, n_gx),
            "gy": lax.rem(b + offset[1] + n_gy, n_gy),
        }

    for offset in DIAGONALS:
        signal(grid_peer(offset))

    load_linv = pltpu.make_async_copy(linv_hbm, linv, load_sem.at[0])
    load_schur = pltpu.make_async_copy(schur_hbm, schur, load_sem.at[1])
    load_linv.start()
    load_schur.start()

    def remote(src, dst, send, recv, device):
        return pltpu.make_async_remote_copy(
            src_ref=src,
            dst_ref=dst,
            send_sem=send,
            recv_sem=recv,
            device_id=device,
            device_id_type=MESH,
        )

    def plane_send(src, dst, send, recv):
        for step in range(n_gy - 1):
            remote(src, dst.at[slot], send, recv, plane_peer(step, 0)).start()
            remote(src, dst.at[slot], send, recv, plane_peer(step, 1)).start()

        remote(src, dst.at[slot], send, recv, plane_peer(n_gy - 1, 1)).start()

    def z_send(src, dst, send, recv):
        for step in range(n_z - 1):
            other = line_peer(step)
            remote(
                src.at[other], dst.at[z], send, recv, {"gx": 2 * other + c, "gy": b}
            ).start()

    def wait_bytes(buf, count, sem):
        part = buf.at[pl.ds(0, count)]
        pltpu.make_async_copy(part, part, sem).wait()

    west = {"gx": lax.rem(a + n_gx - 1, n_gx), "gy": b}
    east = {"gx": lax.rem(a + 1, n_gx), "gy": b}
    south = {"gx": a, "gy": lax.rem(b + n_gy - 1, n_gy)}
    north = {"gx": a, "gy": lax.rem(b + 1, n_gy)}
    neighbours = ((west, 1), (east, 0), (south, 3), (north, 2))

    def face_rows(which):
        return pl.ds(which * face, face)

    def exchange(src, dst, send, recv, faces=(0, 1, 2, 3)):
        copies = []
        for mine in faces:
            device, theirs = neighbours[mine]
            copies.append(
                remote(
                    src.at[face_rows(mine)],
                    dst.at[face_rows(theirs)],
                    send.at[mine],
                    recv.at[theirs],
                    device,
                )
            )
        for copy in copies:
            copy.start()
        return copies

    def finish(copies):
        for copy in copies:
            copy.wait_recv()

    lane = lax.broadcasted_iota(jnp.int32, (1, local), 1)
    which = lane // face
    node = lax.rem(lax.rem(lane, face), nodes_per)
    alive_east = (which == 1) & (node < nodes[0]) & (a < n_gx - 1)
    alive_north = (which == 3) & (node < nodes[1]) & (b < n_gy - 1)
    mask_row = jnp.where(alive_east | alive_north, 1.0, 0.0).astype(F32)
    basis_wide = basis[...].astype(F32)
    n_primal = basis_wide.shape[0]

    bpad[...] = jnp.zeros_like(bpad)
    bpad[TILE : TILE + n_primal, :] = basis_wide
    bpad[MASK_LANE : MASK_LANE + 1, :] = mask_row
    flipped = bpad[...].T
    bt_send[...] = flipped.astype(BF16)
    masks[...] = jnp.broadcast_to(flipped[:, MASK_LANE : MASK_LANE + 1], masks.shape)
    bpad[...] = jnp.zeros_like(bpad)
    bpad[0:n_primal, :] = basis_wide
    bb[...] = bpad[...].T.astype(BF16)
    basis16 = bpad[0:TILE, :].astype(BF16)

    rows[face : 2 * face, :] = (
        loads[0:face, :].astype(F32) * masks[face : 2 * face, :]
    ).astype(BF16)
    rows[3 * face :, :] = (
        loads[face:, :].astype(F32) * masks[3 * face :, :]
    ).astype(BF16)

    name_row = lax.broadcasted_iota(jnp.int32, name_msg.shape, 0)
    name_lane = lax.broadcasted_iota(jnp.int32, name_msg.shape, 1)
    names = CODE + name_row - n_primal
    for j in range(n_primal):
        names = jnp.where(name_row == j, index[j], names)
    half = name_msg.shape[1] // 2
    name_msg[...] = (
        jnp.where(name_lane < half, names // 64, lax.rem(names, 64)).astype(F32).astype(BF16)
    )
    name_plane[slot] = name_msg[...]
    name_gx[c * n_z + z] = name_msg[...]

    half_cr = cr // 2
    row_y, row_x = b // side, lax.rem(b, side)
    wide = jnp.concatenate(
        [cinv[...].astype(BF16), jnp.zeros((cr, strip_w - cc), BF16)], axis=1
    )
    strip_x[b] = wide[:half_cr]
    strip_y[row_x * side + row_y] = wide[half_cr:]

    pl.semaphore_wait(barrier, n_plane - 1 + n_gx - 2 + len(DIAGONALS))

    start_copies = []
    for mine, (device, theirs) in ((1, (east, 0)), (3, (north, 2))):
        copy = remote(
            rows.at[face_rows(mine)],
            rows.at[face_rows(theirs)],
            face_send.at[mine],
            face_recv.at[theirs],
            device,
        )
        copy.start()
        start_copies.append(copy)

    plane_send(name_msg, name_plane, name_send.at[0], name_recv.at[0])

    @pl.loop(1, n_gx)
    def _(k):
        other = lax.rem(a + k, n_gx)
        remote(
            name_msg,
            name_gx.at[c * n_z + z],
            name_send.at[1],
            name_recv.at[1],
            {"gx": other, "gy": b},
        ).start()

    def along_x(step):
        x = lax.rem(row_x + far_first(step, side), side)
        return {"gx": a, "gy": row_y * side + x}

    def along_y(step):
        y = lax.rem(row_y + far_first(step, side), side)
        return {"gx": a, "gy": y * side + row_x}

    def strip_pass(which, first_x, count_x, first_y, count_y):
        here_x = strip_x.at[pl.ds(first_x, count_x)]
        here_y = strip_y.at[pl.ds(first_y, count_y)]
        ways = (along_x, along_y) if which == 0 else (along_y, along_x)

        @pl.loop(0, side - 1)
        def _(step):
            at = 2 * which
            remote(here_x, here_x, strip_send.at[at], strip_recv.at[at], ways[0](step)).start()
            remote(
                here_y, here_y, strip_send.at[at + 1], strip_recv.at[at + 1], ways[1](step)
            ).start()

    def strip_wait(which, sem):
        count = (side - 1) * (side if which else 1)
        wait_bytes(strip_x, count, sem.at[2 * which])
        wait_bytes(strip_y, count, sem.at[2 * which + 1])

    strip_pass(0, b, 1, row_x * side + row_y, 1)

    def coarse_start(k, local_rows, sums):
        primal = jnp.dot(basis16, local_rows, preferred_element_type=F32)
        for j, value in enumerate(sums):
            at = lax.broadcasted_iota(jnp.int32, primal.shape, 0) == n_primal + j
            primal = jnp.where(at, value, primal)
        message = primal.astype(BF16)
        g_msg[k] = message
        g_buf[k, slot] = message
        plane_send(g_msg.at[k], g_buf.at[k], stage_send.at[k, 0], stage_recv.at[k, 0])
        if k == 0:
            strip_wait(0, strip_recv)
            strip_pass(1, row_y * side, side, row_x * side, side)
        t_val[k] = jnp.dot(linv[...], local_rows, preferred_element_type=F32)

    def local_start(k):
        faces = (0, 1, 2, 3) if k + 1 < SOLVES else (0, 2)
        return exchange(t_val.at[k], t_recv.at[k], t_ssem.at[k], t_rsem.at[k], faces)

    def operate(k):
        finish(t_copies[k])
        joined = (t_val[k] + t_recv[k]) * masks[...]
        t_hat[k] = joined
        high = joined.astype(BF16)
        rest = (joined - high.astype(F32)).astype(BF16)
        s_val[k] = jnp.dot(schur[...], high, preferred_element_type=F32) + jnp.dot(
            schur[...], rest, preferred_element_type=F32
        )
        return exchange(s_val.at[k], s_recv.at[k], s_ssem.at[k], s_rsem.at[k])

    def operated(k):
        finish(s_copies[k])
        s_hat[k] = (s_val[k] + s_recv[k]) * masks[...]

    def coarse_scatter(k):
        wait_bytes(g_buf.at[k], n_plane - 1, stage_recv.at[k, 0])
        gathered = g_buf[k].reshape(n_plane * TILE, load_cases)
        part = jnp.dot(sel_t[...], gathered, preferred_element_type=F32)
        part = part.reshape(n_z, 8, load_cases)
        xs[k] = part
        xr[k, z] = xs[k, z]
        z_send(xs.at[k], xr.at[k], stage_send.at[k, 1], stage_recv.at[k, 1])

    def coarse_gather(k):
        wait_bytes(xr.at[k], n_z - 1, stage_recv.at[k, 1])
        mine = jnp.sum(xr[k], axis=0)
        x_msg[k] = mine
        xb[k, slot] = mine
        plane_send(x_msg.at[k], xb.at[k], stage_send.at[k, 2], stage_recv.at[k, 2])

    def coarse_solve(k):
        wait_bytes(xb.at[k], n_plane - 1, stage_recv.at[k, 2])
        low = xb[k, 0:n_gy].reshape(strip_w, load_cases).astype(BF16)
        high = xb[k, n_gy:].reshape(strip_w, load_cases).astype(BF16)
        part = jnp.dot(c2[0], low, preferred_element_type=F32) + jnp.dot(
            c2[1], high, preferred_element_type=F32
        )
        ys[k] = part.astype(BF16).reshape(n_z, TILE, load_cases)
        yr[k, z] = ys[k, z]
        z_send(ys.at[k], yr.at[k], stage_send.at[k, 3], stage_recv.at[k, 3])

    def coarse_direct(k):
        wait_bytes(g_buf.at[k], n_plane - 1, stage_recv.at[k, 0])
        gathered = g_buf[k].reshape(n_plane * TILE, load_cases)
        part = jnp.dot(c_full[...], gathered, preferred_element_type=F32)
        at = lax.rem(lax.broadcasted_iota(jnp.int32, part.shape, 0), TILE)
        rest = part - part.astype(BF16).astype(F32)
        part = jnp.where((at == n_primal + 1) | (at == n_primal + 3), rest, part)
        ys[k] = part.astype(BF16).reshape(n_z, TILE, load_cases)
        yr[k, z] = ys[k, z]
        z_send(ys.at[k], yr.at[k], stage_send.at[k, 3], stage_recv.at[k, 3])

    def coarse_finish(k):
        wait_bytes(yr.at[k], n_z - 1, stage_recv.at[k, 3])
        total = jnp.sum(yr[k].astype(F32), axis=0)
        pk[k, 0:TILE] = total.astype(BF16)
        offsets = OFFSETS if k + 1 < SOLVES else OFFSETS[:4:2]
        for offset in reversed(OFFSETS):
            if offset in offsets:
                back = OFFSETS.index((-offset[0], -offset[1]))
                remote(
                    pk.at[k, pl.ds(0, TILE)],
                    pk.at[k, pl.ds((1 + back) * TILE, TILE)],
                    p_ssem.at[k],
                    p_rsem.at[k],
                    grid_peer(offset),
                ).start()
        first = total[n_primal : n_primal + 1] + total[n_primal + 1 : n_primal + 2]
        second = total[n_primal + 2 : n_primal + 3] + total[n_primal + 3 : n_primal + 4]
        return len(offsets), first, second

    def wait_tiles(k, count, sem):
        part = pk.at[k, pl.ds(TILE, count * TILE)]
        pltpu.make_async_copy(part, part, sem.at[k]).wait()

    def owned(first, second):
        total = first * second
        east_part = jnp.sum(total[face : 2 * face], axis=0, keepdims=True)
        north_part = jnp.sum(total[3 * face :], axis=0, keepdims=True)
        return east_part + north_part

    def split(value):
        high = value.astype(BF16).astype(F32)
        return high, value - high

    finish(start_copies)
    load_linv.wait()
    t_copies = []
    s_copies = []
    coarse_start(0, rows[...], [])

    wait_bytes(name_plane, n_plane - 1, name_recv.at[0])
    plane_names = name_plane[...].reshape(n_plane * TILE, name_msg.shape[1]).astype(F32)
    plane_names = plane_names[:, 0:1] * 64.0 + plane_names[:, half : half + 1]
    target = lax.broadcasted_iota(jnp.int32, (1, 8 * n_z), 1)
    place = 8 * b + lax.rem(target, 8)
    wanted = jnp.where(place < cc, cc * (2 * (target // 8) + c) + place, CODE + place - cc)
    hits = jnp.where(plane_names == wanted.astype(F32), 1.0, 0.0).astype(F32)
    sel_t[...] = hits.T.astype(BF16)

    coarse_scatter(0)
    bt_copies = exchange(bt_send, bt_recv, face_send.at[pl.ds(4, 4)], face_recv.at[pl.ds(4, 4)])

    t_copies.append(local_start(0))

    wait_bytes(name_gx, n_gx - 1, name_recv.at[1])
    gx_names = name_gx[...].reshape(n_gx * TILE, name_msg.shape[1]).astype(F32)
    gx_names = gx_names[:, 0:1] * 64.0 + gx_names[:, half : half + 1]

    width = c_nat.shape[2]
    face_cols = 3 * n_gy
    lanes = lax.broadcasted_iota(jnp.int32, (TILE, width), 1)
    prim = lax.broadcasted_iota(jnp.int32, (TILE, width), 0)
    within = 3 * b + lax.rem(prim, 3)
    low_face = jnp.where(prim < 3, 0, jnp.where(prim < 6, 1, 3))
    high_face = jnp.where(prim < 6, 2, 4)
    owned_prim = ((prim >= 3) & (prim < 6)) | ((prim >= 9) & (prim < 12))
    low_hit = (lanes == low_face * face_cols + within) & (owned_prim | (prim < 3))
    high_hit = (lanes == high_face * face_cols + within) & owned_prim
    spread_names = jnp.broadcast_to(gx_names, (n_gx * TILE, width)).reshape(
        n_gx, TILE, width
    )
    lane_names = jnp.sum(
        jnp.where(low_hit[None], spread_names[:n_z], 0.0)
        + jnp.where(high_hit[None], spread_names[n_z:], 0.0),
        axis=1,
    )
    name_lane_msg[...] = lane_names
    name_cols[b] = lane_names

    @pl.loop(1, n_gy)
    def _(k):
        remote(
            name_lane_msg,
            name_cols.at[b],
            perm_send.at[0],
            perm_recv.at[0],
            {"gx": a, "gy": lax.rem(b + k, n_gy)},
        ).start()

    strip_wait(1, strip_recv)
    column = lax.broadcasted_iota(jnp.int32, (1, cr), 1)
    second_half = column >= half_cr

    def select(step, total):
        at = 2 * step
        at_x = jnp.where(second_half, cr * (at + 1) + column - half_cr, cr * at + column)
        low = lax.rem(at, side) * side + at // side
        at_y = jnp.where(
            second_half, cr * (low + side) + column, cr * low + column + half_cr
        )
        hit_x = jnp.where(gx_names == at_x.astype(F32), 1.0, 0.0).astype(BF16)
        hit_y = jnp.where(gx_names == at_y.astype(F32), 1.0, 0.0).astype(BF16)
        rows_x = strip_x[pl.ds(at, 2)].reshape(cr, strip_w)
        rows_y = strip_y[pl.ds(at, 2)].reshape(cr, strip_w)
        total = total + jnp.dot(hit_x, rows_x, preferred_element_type=F32)
        return total + jnp.dot(hit_y, rows_y, preferred_element_type=F32)

    chosen = lax.fori_loop(
        0, n_gy // 2, select, jnp.zeros((n_gx * TILE, strip_w), F32)
    )
    tsel[...] = chosen.astype(BF16).reshape(2, n_z * TILE, strip_w)
    c2[c] = tsel[c]
    c2_copy = remote(
        tsel.at[1 - c], c2.at[c], c2_send, c2_recv, {"gx": 2 * z + 1 - c, "gy": b}
    )
    c2_copy.start()
    c_own[a] = tsel[c, pl.ds(pl.multiple_of(z * TILE, TILE), TILE)]

    def send_rows(core, other):
        remote(
            tsel.at[core, pl.ds(pl.multiple_of(other * TILE, TILE), TILE)],
            c_own.at[a],
            perm_send.at[1],
            perm_recv.at[1],
            {"gx": 2 * other + core, "gy": b},
        ).start()

    @pl.loop(0, n_z - 1)
    def _(step):
        other = line_peer(step)
        send_rows(0, other)
        send_rows(1, other)

    send_rows(1 - c, z)

    coarse_gather(0)
    finish(bt_copies)
    bb[...] = bb[...] + bt_recv[...]
    masks[0:face, :] = jnp.broadcast_to(
        bt_recv[0:face, MASK_LANE : MASK_LANE + 1].astype(F32), (face, load_cases)
    )
    masks[2 * face : 3 * face, :] = jnp.broadcast_to(
        bt_recv[2 * face : 3 * face, MASK_LANE : MASK_LANE + 1].astype(F32),
        (face, load_cases),
    )
    load_schur.wait()
    s_copies.append(operate(0))

    from_row = lax.broadcasted_iota(jnp.int32, (BT_LANES, SLOT_LANES), 0)
    to_lane = lax.broadcasted_iota(jnp.int32, (BT_LANES, SLOT_LANES), 1)
    for at in range(4):
        to_slot = jnp.where(from_row < TILE, 0, at + 1)
        hit = (to_lane == TILE * to_slot + lax.rem(from_row, TILE)) & (from_row < 2 * TILE)
        move = jnp.where(hit, 1.0, 0.0).astype(BF16)
        here = face_rows(at)
        moved = jnp.dot(bb[here, :], move, preferred_element_type=F32)
        g_mat[here, :] = jnp.where(masks[here, 0:1] > 0.5, moved, 0.0).astype(BF16)
    image = jnp.dot(schur[...], g_mat[:, 0:BT_LANES], preferred_element_type=F32)
    sg_send[...] = image.astype(BF16)
    sg_copies = exchange(sg_send, sg_recv, sg_ssem, sg_rsem)

    c2_copy.wait_recv()
    coarse_solve(0)

    wait_bytes(name_cols, n_gy - 1, perm_recv.at[0])
    col_names = jnp.sum(name_cols[...], axis=0)
    used = lax.broadcasted_iota(jnp.int32, col_names.shape, 1) < 5 * face_cols
    col_strip = ((col_names + 0.5) * (1.0 / cc)).astype(jnp.int32)
    col_low = col_names.astype(jnp.int32) - cc * col_strip
    tau_strip[...] = col_strip
    tau_low[...] = jnp.where(used, col_low, -1)
    wait_bytes(c_own, n_gx - 1, perm_recv.at[1])
    inner = lax.broadcasted_iota(jnp.int32, (strip_w, 1), 0)
    strips = lax.broadcasted_iota(jnp.int32, (n_gx, 1, 1), 0)

    @pl.loop(0, n_z)
    def _(step):
        picks = jnp.where(inner == tau_low[pl.ds(step, 1), :], 1.0, 0.0).astype(BF16)
        mine = c_own[...].reshape(n_gx * TILE, strip_w)
        wide_rows = jnp.dot(mine, picks, preferred_element_type=F32)
        wide_rows = wide_rows.reshape(n_gx, TILE, width)
        hit = strips == tau_strip[pl.ds(step, 1), :][None]
        c_nat[step] = jnp.sum(jnp.where(hit, wide_rows, 0.0), axis=0).astype(BF16)

    c_line[z] = c_nat[z]
    z_send(c_nat, c_line, perm_send.at[2], perm_recv.at[2])

    finish(sg_copies)
    for at in range(4):
        to_slot = jnp.full(from_row.shape, -1, jnp.int32)
        for mine, theirs in enumerate(SEEN[at]):
            to_slot = jnp.where(from_row // TILE == mine, theirs, to_slot)
        hit = to_lane == TILE * to_slot + lax.rem(from_row, TILE)
        move = jnp.where(hit & (to_slot >= 0), 1.0, 0.0).astype(BF16)
        here = face_rows(at)
        moved = jnp.dot(sg_recv[here, :], move, preferred_element_type=F32)
        stay = jnp.where(to_lane == from_row, 1.0, 0.0).astype(BF16)
        kept = jnp.dot(sg_send[here, :], stay, preferred_element_type=F32)
        h_mat[here, :] = jnp.where(masks[here, 0:1] > 0.5, moved + kept, 0.0).astype(BF16)
    operated(0)

    counts = [coarse_finish(0)[0]]
    wait_tiles(0, counts[0], p_rsem)
    first = t_hat[0] + jnp.dot(g_mat[...], pk[0], preferred_element_type=F32)
    image = s_hat[0] + jnp.dot(h_mat[...], pk[0], preferred_element_type=F32)
    v0[...] = first
    w0[...] = image
    start = rows[...].astype(F32)
    old, curve = owned(start, first), owned(first, image)

    coarse_start(1, image.astype(BF16), [*split(old), *split(curve)])
    t_copies.append(local_start(1))

    wait_bytes(c_line, n_z - 1, perm_recv.at[2])
    at = lax.broadcasted_iota(jnp.int32, (1, n_plane * TILE), 1)
    at_slot, at_prim = at // TILE, lax.rem(at, TILE)
    at_core, at_b = at_slot // n_gy, lax.rem(at_slot, n_gy)
    at_face = jnp.where(
        at_prim < 3, at_core, jnp.where(at_prim < 6, 1 + at_core, 3 + at_core)
    )
    at_b = jnp.where((at_prim >= 6) & (at_prim < 9), lax.rem(at_b + n_gy - 1, n_gy), at_b)
    at_col = jnp.where(
        at_prim < 12, at_face * face_cols + 3 * at_b + lax.rem(at_prim, 3), -1
    )
    place = jnp.where(
        lax.broadcasted_iota(jnp.int32, (width, 1), 0) == at_col, 1.0, 0.0
    ).astype(BF16)
    block = jnp.dot(
        c_line[...].reshape(n_z * TILE, width), place, preferred_element_type=F32
    )
    row_prim = lax.rem(lax.broadcasted_iota(jnp.int32, (n_z * TILE, 1), 0), TILE)
    adds = (row_prim >= 12) & (at_prim >= 12) & (row_prim // 2 == at_prim // 2)
    c_full[...] = jnp.where(adds, 1.0, block).astype(BF16)

    coarse_direct(1)
    s_copies.append(operate(1))
    count, old, curve = coarse_finish(1)
    step = old / curve
    counts.append(count)
    operated(1)
    wait_tiles(1, count, p_rsem)
    part = t_hat[1] + jnp.dot(g_mat[...], pk[1], preferred_element_type=F32)
    v1[...] = part
    second = v0[...] - step * part
    z1[...] = second
    image = s_hat[1] + jnp.dot(h_mat[...], pk[1], preferred_element_type=F32)
    image = w0[...] - step * image
    residual = rows[...].astype(F32) - step * w0[...]
    new, second_curve = owned(residual, second), owned(second, image)

    coarse_start(2, image.astype(BF16), [*split(new), *split(second_curve)])
    coarse_direct(2)
    t_copies.append(local_start(2))
    finish(t_copies[2])
    count, new, second_curve = coarse_finish(2)
    ratio = new / old
    step_two = new / (second_curve - ratio * ratio * curve)
    counts.append(count)
    wait_tiles(2, count, p_rsem)
    for half_at, at in enumerate((1, 3)):
        here = face_rows(at)
        there = pl.ds(half_at * face, face)
        part = (t_val[2, here, :] + t_recv[2, here, :]) * masks[here, :] + jnp.dot(
            g_mat[here, :], pk[2], preferred_element_type=F32
        )
        second = z1[here, :]
        direction = second + ratio * v0[here, :]
        sol_out[there, :] = step * v0[here, :] + step_two * direction
        pre_out[there, :] = second - step_two * (part + ratio * v1[here, :])

    for copy in start_copies + bt_copies + [c2_copy] + sg_copies:
        copy.wait_send()
    wait_bytes(name_plane, n_plane - 1, name_send.at[0])
    wait_bytes(name_gx, n_gx - 1, name_send.at[1])
    strip_wait(0, strip_send)
    strip_wait(1, strip_send)
    wait_bytes(name_cols, n_gy - 1, perm_send.at[0])
    wait_bytes(c_own, n_gx - 1, perm_send.at[1])
    wait_bytes(c_line, n_z - 1, perm_send.at[2])
    wait_bytes(xr.at[0], n_z - 1, stage_send.at[0, 1])
    wait_bytes(xb.at[0], n_plane - 1, stage_send.at[0, 2])
    for k in range(SOLVES):
        for copy in t_copies[k]:
            copy.wait_send()
        wait_tiles(k, counts[k], p_ssem)
        wait_bytes(g_buf.at[k], n_plane - 1, stage_send.at[k, 0])
        wait_bytes(yr.at[k], n_z - 1, stage_send.at[k, 3])
    for k in range(OPS):
        for copy in s_copies[k]:
            copy.wait_send()


def shards(
    n_gx, n_gy, loads, schur, local_inv, coarse_basis, coarse_index, face_nodes, coarse_inverse
):
    owned, cases = loads.shape[2:]
    local = schur.shape[-1]
    cr, cc = coarse_inverse.shape
    n_z = n_gx // 2
    n_plane = 2 * n_gy
    strip_w = 8 * n_gy
    dma = pltpu.SemaphoreType.DMA
    vmem = pl.BlockSpec(memory_space=pltpu.VMEM)
    smem = pl.BlockSpec(memory_space=pltpu.SMEM)
    anywhere = pl.BlockSpec(memory_space=pl.ANY)
    scratch = [
        pltpu.VMEM((local, local), BF16),
        pltpu.VMEM((local, local), BF16),
        pltpu.VMEM((BT_LANES, local), F32),
        pltpu.VMEM((local, BT_LANES), BF16),
        pltpu.VMEM((local, BT_LANES), BF16),
        pltpu.VMEM((local, BT_LANES), BF16),
        pltpu.VMEM((local, cases), F32),
        pltpu.VMEM((local, cases), BF16),
        pltpu.VMEM((TILE, 128), BF16),
        pltpu.VMEM((n_plane, TILE, 128), BF16),
        pltpu.VMEM((n_gx, TILE, 128), BF16),
        pltpu.VMEM((8 * n_z, n_plane * TILE), BF16),
        pltpu.VMEM((n_gy, cr // 2, strip_w), BF16),
        pltpu.VMEM((n_gy, cr // 2, strip_w), BF16),
        pltpu.VMEM((2, n_z * TILE, strip_w), BF16),
        pltpu.VMEM((2, n_z * TILE, strip_w), BF16),
        pltpu.VMEM((n_gx, TILE, strip_w), BF16),
        pltpu.VMEM((n_gy, n_z, 16 * n_gy), F32),
        pltpu.VMEM((n_z, 16 * n_gy), F32),
        pltpu.VMEM((n_z, 16 * n_gy), jnp.int32),
        pltpu.VMEM((n_z, 16 * n_gy), jnp.int32),
        pltpu.VMEM((n_z, TILE, 16 * n_gy), BF16),
        pltpu.VMEM((n_z, TILE, 16 * n_gy), BF16),
        pltpu.VMEM((n_z * TILE, n_plane * TILE), BF16),
        pltpu.VMEM((SOLVES, local, cases), F32),
        pltpu.VMEM((SOLVES, local, cases), F32),
        pltpu.VMEM((OPS, local, cases), F32),
        pltpu.VMEM((OPS, local, cases), F32),
        pltpu.VMEM((OPS, local, cases), F32),
        pltpu.VMEM((OPS, local, cases), F32),
        pltpu.VMEM((local, BT_LANES), BF16),
        pltpu.VMEM((local, BT_LANES), BF16),
        pltpu.VMEM((local, SLOT_LANES), BF16),
        pltpu.VMEM((local, SLOT_LANES), BF16),
        pltpu.VMEM((SOLVES, TILE, cases), BF16),
        pltpu.VMEM((SOLVES, n_plane, TILE, cases), BF16),
        pltpu.VMEM((SOLVES, n_z, 8, cases), F32),
        pltpu.VMEM((SOLVES, n_z, 8, cases), F32),
        pltpu.VMEM((SOLVES, 8, cases), F32),
        pltpu.VMEM((SOLVES, n_plane, 8, cases), F32),
        pltpu.VMEM((SOLVES, n_z, TILE, cases), BF16),
        pltpu.VMEM((SOLVES, n_z, TILE, cases), BF16),
        pltpu.VMEM((SOLVES, SLOT_LANES, cases), BF16),
        pltpu.VMEM((local, cases), F32),
        pltpu.VMEM((local, cases), F32),
        pltpu.VMEM((local, cases), F32),
        pltpu.VMEM((local, cases), F32),
        dma((2,)),
        dma((8,)),
        dma((8,)),
        dma((2,)),
        dma((2,)),
        dma((4,)),
        dma((4,)),
        dma,
        dma,
        dma((3,)),
        dma((3,)),
        dma((SOLVES, 4)),
        dma((SOLVES, 4)),
        dma((SOLVES, 4)),
        dma((SOLVES, 4)),
        dma((OPS, 4)),
        dma((OPS, 4)),
        dma((4,)),
        dma((4,)),
        dma((SOLVES,)),
        dma((SOLVES,)),
    ]
    solution, precond = pl.pallas_call(
        functools.partial(kernel, n_gx, n_gy),
        out_shape=(
            jax.ShapeDtypeStruct((owned, cases), F32),
            jax.ShapeDtypeStruct((owned, cases), F32),
        ),
        in_specs=[vmem, anywhere, anywhere, vmem, smem, smem, vmem],
        out_specs=(vmem, vmem),
        scratch_shapes=scratch,
        compiler_params=pltpu.CompilerParams(
            collective_id=0, has_side_effects=True, vmem_limit_bytes=60 * 1024 * 1024
        ),
        name="bddc_cg",
    )(
        loads[0, 0],
        schur[0, 0],
        local_inv[0, 0],
        coarse_basis[0, 0],
        coarse_index[0, 0],
        face_nodes[0, 0],
        coarse_inverse,
    )
    return solution[None, None], precond[None, None]


def solution(mesh):
    placed = (
        P("gx", "gy", None, None),
        P("gx", "gy", None, None),
        P("gx", "gy", None, None),
        P("gx", "gy", None, None),
        P("gx", "gy", None),
        P("gx", "gy", None),
        P("gy", "gx"),
    )
    return jax.shard_map(
        functools.partial(shards, mesh.shape["gx"], mesh.shape["gy"]),
        mesh=mesh,
        in_specs=placed,
        out_specs=(P("gx", "gy", None, None), P("gx", "gy", None, None)),
        check_vma=False,
    )
```
